256 devices in a mesh: dp: 32 (over y, x, core), expert: 8 (over z).
Axes of the slice: x: 4, y: 4, z: 8, core: 2. Of those that a mesh axis runs over, the one named last changes fastest.
Arguments:
- gradients: bfloat16 [8, 8, 3584, 1024], P('expert', None, 'dp')
- owners: int32 [8, 8], P('expert'), may hold values from 0 to 7, as said below
Outputs:
- update: bfloat16 [8, 8, 3584, 1024], P('expert', None, 'dp')
- rms_table: float32 [8, 8], replicated
- owned_rms: float32 [8, 32], P('expert', 'dp')
The draws below stay inside these ranges and needn't reach their ends.
Inputs may be any that keep to these rules, and one draw needn't show every extreme that they name: Entry [g, j] is the team that orthogonalizes matrix j of group g; team t is the devices 4 t to 4 t + 3 along dp. Each row owners[g] is a permutation of the 8 teams.
All inputs are finite; a program needn't handle non-finite values.
Results may differ from the reference program's by a relative error of at most 0.0067.
Values may be sent and summed in bfloat16 or wider, within the bound.
A program may use at most 64 MiB of HBM per device.

```python
import math
import jax
import jax.numpy as jnp
from jax import lax

ROWS = 3584
COLS = 1024
ITERS = 2
GROUPS = 8
TEAMS = 8
MAT_GRP = 8
N_DP = 32


def draw_gradients(key, part):
    key = jax.random.fold_in(key, 11)
    key_base, key_rows, key_cols = jax.random.split(key, 3)
    shape = (GROUPS, MAT_GRP, ROWS, COLS)
    row_scale = jnp.exp(jax.random.uniform(key_rows, (GROUPS, MAT_GRP, ROWS, 1)) * math.log(10.0))
    col_scale = jnp.exp(jax.random.uniform(key_cols, (GROUPS, MAT_GRP, 1, COLS)) * math.log(10.0))
    ramp = jnp.arange(GROUPS, dtype=jnp.float32) / (GROUPS - 1)
    base = jax.random.normal(key_base, shape)
    growth = jnp.exp(ramp * math.log(3.0))
    values = 0.05 * base * row_scale * col_scale * growth[:, None, None, None]
    return values.astype(jnp.bfloat16)


def draw_owners(key, part):
    key = jax.random.fold_in(key, 23)
    keys = jax.random.split(key, GROUPS)
    orders = jax.vmap(lambda one: jax.random.permutation(one, TEAMS))(keys)
    return orders[:, :MAT_GRP].astype(jnp.int32)


def setup_inputs(seed: int = 0) -> dict:
    key_of = jax.random.split(jax.random.key(seed), 3)
    return {
        "gradients": draw_gradients(jax.random.fold_in(key_of[2], 71), 0),
        "owners": draw_owners(jax.random.fold_in(key_of[2], 71), 0),
    }


COEF_A = 3.4445
COEF_B = -4.775
COEF_C = 2.0315

def quarter_gram(matrix):
    blocks = matrix.reshape(N_DP, 4, ROWS // N_DP // 4, COLS)
    parts = []
    for quarter in range(4):
        rows = blocks[:, quarter].reshape(-1, COLS)
        parts.append(jnp.dot(rows.T, rows, preferred_element_type=jnp.float32).astype(jnp.bfloat16))
    lower = (parts[0].astype(jnp.float32) + parts[1].astype(jnp.float32)).astype(jnp.bfloat16)
    upper = (parts[2].astype(jnp.float32) + parts[3].astype(jnp.float32)).astype(jnp.bfloat16)
    return lower.astype(jnp.float32) + upper.astype(jnp.float32)

def orthogonalize(grad):
    gram = quarter_gram(grad)
    trace_sq = jnp.trace(gram)
    scale = 1.0 / jnp.sqrt(trace_sq + 1e-06)
    current = (grad.astype(jnp.float32) * scale).astype(jnp.bfloat16)
    gram = gram * (scale * scale)
    combined = current.astype(jnp.float32)
    for step in range(ITERS):
        if step > 0:
            gram = quarter_gram(current)
        gram_low = gram.astype(jnp.bfloat16)
        first = jnp.dot(current, gram_low, preferred_element_type=jnp.float32).astype(jnp.bfloat16)
        second = jnp.dot(first, gram_low, preferred_element_type=jnp.float32)
        combined = COEF_A * current.astype(jnp.float32) + COEF_B * first.astype(jnp.float32) + COEF_C * second
        if step + 1 < ITERS:
            current = combined.astype(jnp.bfloat16)
    update = (math.sqrt(ROWS) * combined).astype(jnp.bfloat16)
    rms = jnp.sqrt(trace_sq / (ROWS * COLS))
    return (update, rms)

def reference(gradients, owners):
    updates = []
    values = []
    for group in range(GROUPS):
        for matrix in range(MAT_GRP):
            update, rms = orthogonalize(gradients[group, matrix])
            updates.append(update)
            values.append(rms)
    update = jnp.stack(updates).reshape(GROUPS, MAT_GRP, ROWS, COLS)
    rms_table = jnp.stack(values).reshape(GROUPS, MAT_GRP)
    device_team = (jnp.arange(N_DP) // 4).astype(jnp.int32)
    hits = owners[:, :, None] == device_team[None, None, :]
    owned_rms = lax.optimization_barrier(jnp.sum(jnp.where(hits, rms_table[:, :, None], jnp.zeros((), rms_table.dtype)), axis=1))
    return (update, rms_table, owned_rms)
```

```python
import functools
import math

import jax
import jax.numpy as jnp
from jax import lax
from jax.experimental import pallas as pl
from jax.experimental.pallas import tpu as pltpu
from jax.sharding import PartitionSpec as P

COEF_A = 3.4445
COEF_B = -4.775
COEF_C = 2.0315

RING = 4
BLK = 256
HALF = BLK // 2
PIECE = 2 * BLK + HALF

F32 = jnp.float32
BF16 = jnp.bfloat16


def dot(a, b):
    return lax.dot_general(a, b, (((1,), (0,)), ((), ())), preferred_element_type=F32)


def dot_t(a, b):
    return lax.dot_general(a, b, (((0,), (0,)), ((), ())), preferred_element_type=F32)


def kernel(
    total_rows,
    n_groups,
    g_ref,
    owners_ref,
    u_ref,
    table_ref,
    owned_ref,
    x_ref,
    acc_ref,
    piece_ref,
    rs_ref,
    ag_ref,
    s_ref,
    e1_ref,
    r_ref,
    a1_ref,
    e2_ref,
    e_ref,
    y_ref,
    rms_ref,
    tab_ref,
    local_sem,
    in_send,
    in_recv,
    rs_send,
    rs_recv,
    ag_send,
    ag_recv,
    out_send,
    out_recv,
    rms_send,
    rms_recv,
    tab_send,
    tab_recv,
):
    rows = g_ref.shape[2]
    cols = g_ref.shape[3]
    d = lax.axis_index("dp")
    group = lax.axis_index("expert")
    c = lax.rem(d, 2)
    x = lax.rem(d // 2, RING)
    y = d // (2 * RING)
    p = jnp.where(c == 0, x, y)
    q = jnp.where(c == 0, y, x)
    p_stride = jnp.where(c == 0, 2, 2 * RING)
    q_stride = jnp.where(c == 0, 2 * RING, 2)
    chip = d - c
    mine = c * RING + p

    def along_p(offset, core):
        return chip + (lax.rem(p + offset, RING) - p) * p_stride + core

    def along_q(offset, core):
        return chip + (lax.rem(q + offset, RING) - q) * q_stride + core

    def remote(src, dst, send, recv, dp):
        return pltpu.make_async_remote_copy(
            src_ref=src,
            dst_ref=dst,
            send_sem=send,
            recv_sem=recv,
            device_id=(dp, group),
            device_id_type=pl.DeviceIdType.MESH,
        )

    def remote_group(src, dst, send, recv, other):
        return pltpu.make_async_remote_copy(
            src_ref=src,
            dst_ref=dst,
            send_sem=send,
            recv_sem=recv,
            device_id=(d, other),
            device_id_type=pl.DeviceIdType.MESH,
        )

    barrier = pltpu.get_barrier_semaphore()
    greeted = []
    for offset in range(RING):
        for core in (c, 1 - c):
            if offset == 0 and core is c:
                continue
            greeted.append((along_p(offset, core), group))
    for offset in range(1, RING):
        for core in (c, 1 - c):
            greeted.append((along_q(offset, core), group))
    for offset in range(1, n_groups):
        greeted.append((d, lax.rem(group + offset, n_groups)))
    for who in greeted:
        pl.semaphore_signal(barrier, inc=1, device_id=who, device_id_type=pl.DeviceIdType.MESH)
    own = pltpu.make_async_copy(
        g_ref.at[0, mine], x_ref.at[pl.ds(pl.multiple_of(c * rows, 16), rows)], local_sem.at[0]
    )
    own.start()
    pl.semaphore_wait(barrier, len(greeted))

    def slot(offset, core):
        return x_ref.at[pl.ds(pl.multiple_of((2 * offset + core) * rows, 16), rows)]

    sent = []
    for offset in (2, 1, 3, 0):
        back = (RING - offset) % RING
        index = lax.rem(p + back, RING)
        if offset:
            copy = remote(
                g_ref.at[0, c * RING + index],
                slot(offset, c),
                in_send.at[2 * offset],
                in_recv.at[2 * offset + c],
                along_p(back, c),
            )
            copy.start()
            sent.append(copy)
        index = lax.rem(q + back, RING)
        copy = remote(
            g_ref.at[0, (1 - c) * RING + index],
            slot(offset, c),
            in_send.at[2 * offset + 1],
            in_recv.at[2 * offset + c],
            along_q(back, 1 - c),
        )
        copy.start()
        sent.append(copy)

    def arrive(offset, core):
        remote(
            g_ref.at[0, 0], slot(offset, core), in_send.at[0], in_recv.at[2 * offset + core], d
        ).wait_recv()

    def share(k, first, count):
        chunk = pl.ds(first * rows, count * rows)

        def col(block, width=BLK, off=0):
            return x_ref[chunk, pl.ds(pl.multiple_of(block * BLK + off, 128), width)]

        low = lax.rem(k, 2)
        right = col(k)
        return (
            dot_t(right, right),
            dot_t(col(lax.rem(k + 1, RING)), right),
            dot_t(col(low + 2, HALF, (k // 2) * HALF), col(low)),
        )

    spans = ((0, BLK), (BLK, BLK), (2 * BLK, HALF))

    own.wait()
    arrive(0, 1 - c)

    @pl.loop(0, RING)
    def _(k):
        for (start, size), value in zip(spans, share(k, 0, 2)):
            acc_ref[k, pl.ds(start, size)] = value

    arrive(1, 0)
    arrive(1, 1)

    @pl.loop(0, RING)
    def _(k):
        for (start, size), value in zip(spans, share(k, 2, 2)):
            acc_ref[k, pl.ds(start, size)] += value

    arrive(3, 0)
    arrive(3, 1)

    @pl.loop(0, RING)
    def _(k):
        for (start, size), value in zip(spans, share(k, 6, 2)):
            acc_ref[k, pl.ds(start, size)] += value

    arrive(2, 0)
    arrive(2, 1)

    for offset in (2, 1, 3):
        k = lax.rem(q + offset, RING)
        for (start, size), value in zip(spans, share(k, 4, 2)):
            piece_ref[offset - 1, pl.ds(start, size)] = (
                acc_ref[k, pl.ds(start, size)] + value
            ).astype(BF16)
        copy = remote(
            piece_ref.at[offset - 1],
            rs_ref.at[RING - 1 - offset],
            rs_send.at[offset - 1],
            rs_recv.at[RING - 1 - offset],
            along_q(offset, c),
        )
        copy.start()
        sent.append(copy)
    for (start, size), value in zip(spans, share(q, 4, 2)):
        acc_ref[q, pl.ds(start, size)] += value
    for index in range(RING - 1):
        remote(
            piece_ref.at[0], rs_ref.at[index], rs_send.at[0], rs_recv.at[index], d
        ).wait_recv()
    ag_ref[q] = (
        acc_ref[q]
        + rs_ref[0].astype(F32)
        + rs_ref[1].astype(F32)
        + rs_ref[2].astype(F32)
    ).astype(BF16)
    for offset in (2, 1, 3):
        copy = remote(
            ag_ref.at[q], ag_ref.at[q], ag_send.at[offset - 1], ag_recv.at[q], along_q(offset, c)
        )
        copy.start()
        sent.append(copy)
    for offset in (1, 3, 2):
        k = lax.rem(q + offset, RING)
        remote(ag_ref.at[k], ag_ref.at[k], ag_send.at[0], ag_recv.at[k], d).wait_recv()

    diag = lax.broadcasted_iota(jnp.int32, (BLK, BLK), 0) == lax.broadcasted_iota(
        jnp.int32, (BLK, BLK), 1
    )
    on_diag = jnp.zeros((BLK, BLK), F32)
    for k in range(RING):
        on_diag += jnp.where(diag, ag_ref[k, pl.ds(0, BLK)].astype(F32), 0.0)
    trace = jnp.sum(jnp.sum(on_diag, axis=0, keepdims=True), axis=1, keepdims=True)
    scale = 1.0 / jnp.sqrt(trace + 1e-06)
    rms = jnp.sqrt(trace / (total_rows * cols))
    rms_ref[mine] = jnp.broadcast_to(rms, (8, 128))
    number = 0
    for offset in range(RING):
        for core in (c, 1 - c):
            if offset == 0 and core is c:
                continue
            copy = remote(
                rms_ref.at[mine],
                rms_ref.at[mine],
                rms_send.at[number],
                rms_recv.at[mine],
                along_p(offset, core),
            )
            copy.start()
            sent.append(copy)
            number += 1

    square = scale * scale
    for k in range(RING):
        up = (k + 1) % RING
        low = k % 2
        high = (low + 2) * BLK + (k // 2) * HALF
        one = (ag_ref[k, pl.ds(0, BLK)].astype(F32) * square).astype(BF16)
        s_ref[pl.ds(k * BLK, BLK), pl.ds(k * BLK, BLK)] = one
        one = (ag_ref[k, pl.ds(BLK, BLK)].astype(F32) * square).astype(BF16)
        s_ref[pl.ds(up * BLK, BLK), pl.ds(k * BLK, BLK)] = one
        s_ref[pl.ds(k * BLK, BLK), pl.ds(up * BLK, BLK)] = one.T
        one = (ag_ref[k, pl.ds(2 * BLK, HALF)].astype(F32) * square).astype(BF16)
        s_ref[pl.ds(high, HALF), pl.ds(low * BLK, BLK)] = one
        s_ref[pl.ds(low * BLK, BLK), pl.ds(high, HALF)] = one.T

    for offset in range(1, RING):
        other = c * RING + lax.rem(p + offset, RING)
        remote(rms_ref.at[other], rms_ref.at[other], rms_send.at[0], rms_recv.at[other], d).wait_recv()
    for index in range(RING):
        other = (1 - c) * RING + index
        remote(rms_ref.at[other], rms_ref.at[other], rms_send.at[0], rms_recv.at[other], d).wait_recv()
    lane = lax.broadcasted_iota(jnp.int32, (8, 128), 1)
    line = jnp.zeros((8, 128), F32)
    for index in range(2 * RING):
        line = jnp.where(lane == index, rms_ref[index], line)
    tab_ref[group] = line
    for offset in range(1, n_groups):
        copy = remote_group(
            tab_ref.at[group],
            tab_ref.at[group],
            tab_send.at[offset - 1],
            tab_recv.at[group],
            lax.rem(group + offset, n_groups),
        )
        copy.start()
        sent.append(copy)
    team = d // 4
    owned_ref[...] = jnp.sum(
        jnp.where(owners_ref[...] == team, line[0:1, 0 : 2 * RING], 0.0), axis=1, keepdims=True
    )

    def product(left, right, finish):
        @pl.loop(0, RING)
        def _(i):
            span = pl.ds(pl.multiple_of(i * BLK, BLK), BLK)
            finish(span, dot(left[span, :], right[...]))

    def finish_e1(span, value):
        e1_ref[span, :] = (COEF_B * s_ref[span, :].astype(F32) + COEF_C * value).astype(BF16)

    def finish_r(span, value):
        r_ref[span, :] = (COEF_A * s_ref[span, :].astype(F32) + value).astype(BF16)

    def finish_a1(span, value):
        a1_ref[span, :] = (COEF_A * r_ref[span, :].astype(F32) + value).astype(BF16)

    def finish_e2(span, value):
        e2_ref[span, :] = (COEF_B * a1_ref[span, :].astype(F32) + COEF_C * value).astype(BF16)

    def finish_e(span, value):
        both = e1_ref[span, :].astype(F32) + e2_ref[span, :].astype(F32)
        e_ref[span, :] = (COEF_A * both + value).astype(BF16)

    product(s_ref, s_ref, finish_e1)
    product(e1_ref, s_ref, finish_r)
    product(e1_ref, r_ref, finish_a1)
    product(a1_ref, a1_ref, finish_e2)
    product(e1_ref, e2_ref, finish_e)

    factor = math.sqrt(total_rows) * scale
    for offset in (2, 1, 3, 0):
        chunk = pl.ds(2 * offset * rows, 2 * rows)
        block = x_ref[chunk, :]
        value = COEF_A * COEF_A * block.astype(F32) + dot(block, e_ref[...])
        y_ref[chunk, :] = (factor * value).astype(BF16)
        for core in (0, 1):
            home = y_ref.at[pl.ds((2 * offset + core) * rows, rows)]
            if offset:
                copy = remote(
                    home,
                    u_ref.at[0, mine],
                    out_send.at[2 * offset + core],
                    out_recv.at[mine],
                    along_p(offset, core),
                )
                copy.start()
                sent.append(copy)
    keep = pltpu.make_async_copy(
        y_ref.at[pl.ds(pl.multiple_of(c * rows, 16), rows)], u_ref.at[0, mine], local_sem.at[1]
    )
    keep.start()
    copy = remote(
        y_ref.at[pl.ds(pl.multiple_of((1 - c) * rows, 16), rows)],
        u_ref.at[0, mine],
        out_send.at[0],
        out_recv.at[mine],
        along_p(0, 1 - c),
    )
    copy.start()
    sent.append(copy)

    for offset in range(1, n_groups):
        other = lax.rem(group + offset, n_groups)
        remote_group(
            tab_ref.at[other], tab_ref.at[other], tab_send.at[0], tab_recv.at[other], group
        ).wait_recv()
    sub = lax.broadcasted_iota(jnp.int32, (8, 128), 0)
    whole = jnp.zeros((8, 128), F32)
    for index in range(n_groups):
        whole = jnp.where(sub == index, tab_ref[index], whole)
    table_ref[...] = whole[0:n_groups, 0 : 2 * RING]

    keep.wait()
    for offset in range(1, RING):
        other = c * RING + lax.rem(p + offset, RING)
        remote(
            y_ref.at[pl.ds(0, rows)], u_ref.at[0, other], out_send.at[0], out_recv.at[other], d
        ).wait_recv()
    for index in range(RING):
        other = (1 - c) * RING + index
        remote(
            y_ref.at[pl.ds(0, rows)], u_ref.at[0, other], out_send.at[0], out_recv.at[other], d
        ).wait_recv()
    for copy in sent:
        copy.wait_send()


def body(gradients, owners):
    _, mats, rows, cols = gradients.shape
    n_groups = lax.axis_size("expert")
    total_rows = rows * lax.axis_size("dp")
    any_space = pl.BlockSpec(memory_space=pl.ANY)
    vmem = pl.BlockSpec(memory_space=pltpu.VMEM)
    full = pltpu.VMEM((cols, cols), BF16)
    dma = pltpu.SemaphoreType.DMA
    return pl.pallas_call(
        functools.partial(kernel, total_rows, n_groups),
        out_shape=(
            jax.ShapeDtypeStruct(gradients.shape, BF16),
            jax.ShapeDtypeStruct((n_groups, mats), F32),
            jax.ShapeDtypeStruct((1, 1), F32),
        ),
        in_specs=[any_space, vmem],
        out_specs=(any_space, vmem, vmem),
        scratch_shapes=[
            pltpu.VMEM((mats * rows, cols), BF16),
            pltpu.VMEM((RING, PIECE, BLK), F32),
            pltpu.VMEM((RING - 1, PIECE, BLK), BF16),
            pltpu.VMEM((RING - 1, PIECE, BLK), BF16),
            pltpu.VMEM((RING, PIECE, BLK), BF16),
            full,
            full,
            full,
            full,
            full,
            full,
            pltpu.VMEM((mats * rows, cols), BF16),
            pltpu.VMEM((2 * RING, 8, 128), F32),
            pltpu.VMEM((n_groups, 8, 128), F32),
            dma((2,)),
            dma((2 * RING,)),
            dma((2 * RING,)),
            dma((RING - 1,)),
            dma((RING - 1,)),
            dma((RING - 1,)),
            dma((RING,)),
            dma((2 * RING,)),
            dma((2 * RING,)),
            dma((2 * RING - 1,)),
            dma((2 * RING,)),
            dma((n_groups - 1,)),
            dma((n_groups,)),
        ],
        compiler_params=pltpu.CompilerParams(
            collective_id=0, has_side_effects=True, vmem_limit_bytes=56 * 1024 * 1024
        ),
    )(gradients, owners)


def solution(mesh):
    placed = (P("expert", None, "dp", None), P("expert", None))
    return jax.shard_map(
        body,
        mesh=mesh,
        in_specs=placed,
        out_specs=(P("expert", None, "dp", None), P(), P("expert", "dp")),
        check_vma=False,
    )
```

```python
import functools
import math

import jax
import jax.numpy as jnp
from jax import lax
from jax.experimental import pallas as pl
from jax.experimental.pallas import tpu as pltpu
from jax.sharding import PartitionSpec as P

COEF_A = 3.4445
COEF_B = -4.775
COEF_C = 2.0315

RING = 4
BLK = 256
HALF = BLK // 2
EARLY = 3 * BLK
PIECE = BLK + HALF

F32 = jnp.float32
BF16 = jnp.bfloat16


def dot(a, b):
    return lax.dot_general(a, b, (((1,), (0,)), ((), ())), preferred_element_type=F32)


def dot_t(a, b):
    return lax.dot_general(a, b, (((0,), (0,)), ((), ())), preferred_element_type=F32)


def kernel(
    total_rows,
    n_groups,
    g_ref,
    u_ref,
    whole_ref,
    x_ref,
    pa_ref,
    pb_ref,
    ra_ref,
    rb_ref,
    aa_ref,
    ab_ref,
    tr_ref,
    s_ref,
    e1_ref,
    r_ref,
    a1_ref,
    e2_ref,
    e_ref,
    y_ref,
    rms_ref,
    tab_ref,
    local_sem,
    in_send,
    in_recv,
    rs_send,
    rs_recv,
    ag_send,
    ag_recv,
    tr_send,
    tr_recv,
    out_send,
    out_recv,
    rms_send,
    rms_recv,
    tab_send,
    tab_recv,
):
    rows = g_ref.shape[2]
    cols = g_ref.shape[3]
    d = lax.axis_index("dp")
    group = lax.axis_index("expert")
    c = lax.rem(d, 2)
    x = lax.rem(d // 2, RING)
    y = d // (2 * RING)
    p = jnp.where(c == 0, x, y)
    q = jnp.where(c == 0, y, x)
    p_stride = jnp.where(c == 0, 2, 2 * RING)
    q_stride = jnp.where(c == 0, 2 * RING, 2)
    chip = d - c
    mine = c * RING + p

    def along_p(offset, core):
        return chip + (lax.rem(p + offset, RING) - p) * p_stride + core

    def along_q(offset, core):
        return chip + (lax.rem(q + offset, RING) - q) * q_stride + core

    def remote(src, dst, send, recv, dp, to_group=group):
        return pltpu.make_async_remote_copy(
            src_ref=src,
            dst_ref=dst,
            send_sem=send,
            recv_sem=recv,
            device_id=(dp, to_group),
            device_id_type=pl.DeviceIdType.MESH,
        )

    barrier = pltpu.get_barrier_semaphore()
    greeted = []
    for offset in range(RING):
        for core in (c, 1 - c):
            if offset == 0 and core is c:
                continue
            greeted.append((along_p(offset, core), group))
    for offset in range(1, RING):
        for core in (c, 1 - c):
            greeted.append((along_q(offset, core), group))
    for offset in range(1, n_groups):
        greeted.append((d, lax.rem(group + offset, n_groups)))
    for who in greeted:
        pl.semaphore_signal(barrier, inc=1, device_id=who, device_id_type=pl.DeviceIdType.MESH)
    own = pltpu.make_async_copy(
        g_ref.at[0, mine], x_ref.at[pl.ds(pl.multiple_of(c * rows, 16), rows)], local_sem.at[0]
    )
    own.start()
    pl.semaphore_wait(barrier, len(greeted))

    parts = (pl.ds(0, EARLY), pl.ds(EARLY, cols - EARLY))

    def slot(offset, core, part):
        return x_ref.at[pl.ds(pl.multiple_of((2 * offset + core) * rows, 16), rows), part]

    sent = []
    for number, part in enumerate(parts):
        for offset in (2, 1, 3, 0):
            back = (RING - offset) % RING
            if offset:
                copy = remote(
                    g_ref.at[0, c * RING + lax.rem(p + back, RING), :, part],
                    slot(offset, c, part),
                    in_send.at[number, 2 * offset],
                    in_recv.at[number, 2 * offset + c],
                    along_p(back, c),
                )
                copy.start()
                sent.append(copy)
            copy = remote(
                g_ref.at[0, (1 - c) * RING + lax.rem(q + back, RING), :, part],
                slot(offset, c, part),
                in_send.at[number, 2 * offset + 1],
                in_recv.at[number, 2 * offset + c],
                along_q(back, 1 - c),
            )
            copy.start()
            sent.append(copy)

    def arrive(number):
        part = parts[number]
        for offset, core in ((0, 1 - c), (1, 0), (1, 1), (3, 0), (3, 1), (2, 0), (2, 1)):
            remote(
                g_ref.at[0, 0, :, part],
                slot(offset, core, part),
                in_send.at[number, 0],
                in_recv.at[number, 2 * offset + core],
                d,
            ).wait_recv()

    diag = lax.broadcasted_iota(jnp.int32, (BLK, BLK), 0) == lax.broadcasted_iota(
        jnp.int32, (BLK, BLK), 1
    )

    def on_diag(value):
        return jnp.sum(jnp.where(diag, value, 0.0), axis=0, keepdims=True)

    own.wait()
    arrive(0)
    value = dot_t(x_ref[:, pl.ds(0, BLK)], x_ref[:, pl.ds(0, BLK)])
    total = on_diag(value)
    pa_ref[0, pl.ds(0, BLK)] = value.astype(BF16)
    value = dot_t(x_ref[:, pl.ds(BLK, BLK)], x_ref[:, pl.ds(0, 2 * BLK)])
    total += on_diag(value[:, BLK:])
    pa_ref[0, pl.ds(BLK, HALF)] = value[:HALF, :BLK].astype(BF16)
    pa_ref[1, pl.ds(BLK, HALF)] = value[HALF:, :BLK].astype(BF16)
    pa_ref[1, pl.ds(0, BLK)] = value[:, BLK:].astype(BF16)
    value = dot_t(x_ref[:, pl.ds(2 * BLK, BLK)], x_ref[:, pl.ds(0, 3 * BLK)])
    total += on_diag(value[:, 2 * BLK :])
    pa_ref[2, pl.ds(BLK, HALF)] = value[:HALF, :BLK].astype(BF16)
    pa_ref[3, pl.ds(BLK, HALF)] = value[HALF:, :BLK].astype(BF16)
    pa_ref[3, pl.ds(0, BLK)] = value[:, BLK : 2 * BLK].astype(BF16)
    pa_ref[2, pl.ds(0, BLK)] = value[:, 2 * BLK :].astype(BF16)

    def scatter(number, piece_ref, got_ref):
        for offset in (2, 1, 3):
            copy = remote(
                piece_ref.at[lax.rem(q + offset, RING)],
                got_ref.at[RING - 1 - offset],
                rs_send.at[number, offset - 1],
                rs_recv.at[number, RING - 1 - offset],
                along_q(offset, c),
            )
            copy.start()
            sent.append(copy)

    def add_up(number, piece_ref, got_ref, all_ref):
        for index in range(RING - 1):
            remote(
                piece_ref.at[0], got_ref.at[index], rs_send.at[number, 0], rs_recv.at[number, index], d
            ).wait_recv()
        all_ref[q] = (
            (piece_ref[q].astype(F32) + got_ref[0].astype(F32))
            + (got_ref[1].astype(F32) + got_ref[2].astype(F32))
        ).astype(BF16)
        for offset in (2, 1, 3):
            copy = remote(
                all_ref.at[q],
                all_ref.at[q],
                ag_send.at[number, offset - 1],
                ag_recv.at[number, q],
                along_q(offset, c),
            )
            copy.start()
            sent.append(copy)

    def collect(number, all_ref):
        for offset in (1, 3, 2):
            k = lax.rem(q + offset, RING)
            remote(
                all_ref.at[k], all_ref.at[k], ag_send.at[number, 0], ag_recv.at[number, k], d
            ).wait_recv()

    scatter(0, pa_ref, ra_ref)

    arrive(1)
    value = dot_t(x_ref[:, pl.ds(EARLY, BLK)], x_ref[...])
    total += on_diag(value[:, EARLY:])
    for k in range(RING):
        pb_ref[k] = value[:, k * BLK : (k + 1) * BLK].astype(BF16)
    scatter(1, pb_ref, rb_ref)
    tr_ref[q] = jnp.broadcast_to(jnp.sum(total, axis=1, keepdims=True), (8, 128))
    for offset in (2, 1, 3):
        copy = remote(
            tr_ref.at[q], tr_ref.at[q], tr_send.at[offset - 1], tr_recv.at[q], along_q(offset, c)
        )
        copy.start()
        sent.append(copy)
    add_up(0, pa_ref, ra_ref, aa_ref)
    add_up(1, pb_ref, rb_ref, ab_ref)

    for offset in (1, 3, 2):
        k = lax.rem(q + offset, RING)
        remote(tr_ref.at[k], tr_ref.at[k], tr_send.at[0], tr_recv.at[k], d).wait_recv()
    trace = ((tr_ref[0] + tr_ref[1]) + (tr_ref[2] + tr_ref[3]))[0:1, 0:1]
    scale = 1.0 / jnp.sqrt(trace + 1e-06)
    rms = jnp.sqrt(trace / (total_rows * cols))
    rms_ref[mine] = jnp.broadcast_to(rms, (8, 128))
    number = 0
    for offset in range(RING):
        for core in (c, 1 - c):
            if offset == 0 and core is c:
                continue
            copy = remote(
                rms_ref.at[mine],
                rms_ref.at[mine],
                rms_send.at[number],
                rms_recv.at[mine],
                along_p(offset, core),
            )
            copy.start()
            sent.append(copy)
            number += 1

    square = scale * scale

    def block(i):
        return pl.ds(i * BLK, BLK)

    collect(0, aa_ref)
    for k, (i, j) in enumerate(((0, 0), (1, 1), (2, 2), (2, 1))):
        one = (aa_ref[k, pl.ds(0, BLK)].astype(F32) * square).astype(BF16)
        s_ref[block(i), block(j)] = one
        if i != j:
            s_ref[block(j), block(i)] = one.T
        high = pl.ds((1 + k // 2) * BLK + (k % 2) * HALF, HALF)
        one = (aa_ref[k, pl.ds(BLK, HALF)].astype(F32) * square).astype(BF16)
        s_ref[high, block(0)] = one
        s_ref[block(0), high] = one.T
    collect(1, ab_ref)
    for k in range(RING):
        one = (ab_ref[k].astype(F32) * square).astype(BF16)
        s_ref[block(3), block(k)] = one
        if k < 3:
            s_ref[block(k), block(3)] = one.T

    def product(out_ref, left, right, plus, by, times):
        for i in range(RING):
            wide = pl.ds(0, (i + 1) * BLK)
            value = by * plus[block(i), wide].astype(F32) + times * dot(
                left[block(i), :], right[:, wide]
            )
            value = value.astype(BF16)
            out_ref[block(i), wide] = value
            for j in range(i):
                out_ref[block(j), block(i)] = value[:, j * BLK : (j + 1) * BLK].T

    product(e1_ref, s_ref, s_ref, s_ref, COEF_B, COEF_C)

    for offset in range(1, RING):
        other = c * RING + lax.rem(p + offset, RING)
        remote(rms_ref.at[other], rms_ref.at[other], rms_send.at[0], rms_recv.at[other], d).wait_recv()
    for index in range(RING):
        other = (1 - c) * RING + index
        remote(rms_ref.at[other], rms_ref.at[other], rms_send.at[0], rms_recv.at[other], d).wait_recv()
    lane = lax.broadcasted_iota(jnp.int32, (8, 128), 1)
    line = jnp.zeros((8, 128), F32)
    for index in range(2 * RING):
        line = jnp.where(lane == index, rms_ref[index], line)
    tab_ref[group] = line
    for offset in range(1, n_groups):
        copy = remote(
            tab_ref.at[group],
            tab_ref.at[group],
            tab_send.at[offset - 1],
            tab_recv.at[group],
            d,
            lax.rem(group + offset, n_groups),
        )
        copy.start()
        sent.append(copy)

    product(r_ref, e1_ref, s_ref, s_ref, COEF_A, 1.0)
    product(a1_ref, e1_ref, r_ref, r_ref, COEF_A, 1.0)
    product(e2_ref, a1_ref, a1_ref, a1_ref, COEF_B, COEF_C)

    factor = math.sqrt(total_rows) * scale
    for n in range(RING):
        both = e1_ref[:, block(n)].astype(F32) + e2_ref[:, block(n)].astype(F32)
        e_ref[:, block(n)] = (COEF_A * both + dot(e1_ref[...], e2_ref[:, block(n)])).astype(BF16)
        value = COEF_A * COEF_A * x_ref[:, block(n)].astype(F32) + dot(
            x_ref[...], e_ref[:, block(n)]
        )
        y_ref[:, block(n)] = (factor * value).astype(BF16)

        def home(offset, core):
            return y_ref.at[
                pl.ds(pl.multiple_of((2 * offset + core) * rows, 16), rows), block(n)
            ]

        for offset, core in ((2, 0), (2, 1), (1, 0), (1, 1), (3, 0), (3, 1), (0, 1 - c)):
            remote(
                home(offset, core),
                u_ref.at[mine, :, block(n)],
                out_send.at[2 * offset + core],
                out_recv.at[mine],
                along_p(offset, core),
            ).start()
        pltpu.make_async_copy(home(0, c), u_ref.at[mine, :, block(n)], local_sem.at[1]).start()

    for offset in range(1, n_groups):
        other = lax.rem(group + offset, n_groups)
        remote(
            tab_ref.at[other], tab_ref.at[other], tab_send.at[0], tab_recv.at[other], d
        ).wait_recv()
    sub = lax.broadcasted_iota(jnp.int32, (8, 128), 0)
    whole = jnp.zeros((8, 128), F32)
    for index in range(n_groups):
        whole = jnp.where(sub == index, tab_ref[index], whole)
    whole_ref[...] = whole

    def all_columns(other, offset, core):
        return remote(
            y_ref.at[pl.ds(pl.multiple_of((2 * offset + core) * rows, 16), rows)],
            u_ref.at[other],
            out_send.at[2 * offset + core],
            out_recv.at[other],
            d,
        )

    pltpu.make_async_copy(y_ref.at[pl.ds(0, rows)], u_ref.at[mine], local_sem.at[1]).wait()
    for offset in range(1, RING):
        all_columns(c * RING + lax.rem(p + offset, RING), 0, 0).wait_recv()
    for index in range(RING):
        all_columns((1 - c) * RING + index, 0, 0).wait_recv()
    for offset, core in ((2, 0), (2, 1), (1, 0), (1, 1), (3, 0), (3, 1), (0, 1 - c)):
        all_columns(mine, offset, core).wait_send()
    for copy in sent:
        copy.wait_send()


def finish(n_groups, u_ref, whole_ref, owners_ref, update_ref, table_ref, owned_ref, sem):
    mats = u_ref.shape[0]
    copies = [
        pltpu.make_async_copy(u_ref.at[m], update_ref.at[0, m], sem.at[m]) for m in range(mats)
    ]
    for copy in copies:
        copy.start()
    table = whole_ref[...][0:n_groups, 0:mats]
    table_ref[...] = table
    sub = lax.broadcasted_iota(jnp.int32, table.shape, 0)
    mask = (sub == lax.axis_index("expert")) & (owners_ref[...] == lax.axis_index("dp") // 4)
    hit = jnp.sum(jnp.where(mask, table, 0.0), axis=0, keepdims=True)
    owned_ref[...] = jnp.sum(hit, axis=1, keepdims=True)
    for copy in copies:
        copy.wait()


def body(gradients, owners):
    _, mats, rows, cols = gradients.shape
    n_groups = lax.axis_size("expert")
    total_rows = rows * lax.axis_size("dp")
    any_space = pl.BlockSpec(memory_space=pl.ANY)
    vmem = pl.BlockSpec(memory_space=pltpu.VMEM)
    full = pltpu.VMEM((cols, cols), BF16)
    dma = pltpu.SemaphoreType.DMA
    early = (PIECE, BLK)
    late = (BLK, BLK)
    moved, whole = pl.pallas_call(
        functools.partial(kernel, total_rows, n_groups),
        out_shape=(
            pltpu.VMEM((mats, rows, cols), BF16),
            jax.ShapeDtypeStruct((8, 128), F32),
        ),
        in_specs=[any_space],
        out_specs=(vmem, vmem),
        scratch_shapes=[
            pltpu.VMEM((mats * rows, cols), BF16),
            pltpu.VMEM((RING, *early), BF16),
            pltpu.VMEM((RING, *late), BF16),
            pltpu.VMEM((RING - 1, *early), BF16),
            pltpu.VMEM((RING - 1, *late), BF16),
            pltpu.VMEM((RING, *early), BF16),
            pltpu.VMEM((RING, *late), BF16),
            pltpu.VMEM((RING, 8, 128), F32),
            full,
            full,
            full,
            full,
            full,
            full,
            pltpu.VMEM((mats * rows, cols), BF16),
            pltpu.VMEM((2 * RING, 8, 128), F32),
            pltpu.VMEM((n_groups, 8, 128), F32),
            dma((2,)),
            dma((2, 2 * RING)),
            dma((2, 2 * RING)),
            dma((2, RING - 1)),
            dma((2, RING - 1)),
            dma((2, RING - 1)),
            dma((2, RING)),
            dma((RING - 1,)),
            dma((RING,)),
            dma((2 * RING,)),
            dma((2 * RING,)),
            dma((2 * RING - 1,)),
            dma((2 * RING,)),
            dma((n_groups - 1,)),
            dma((n_groups,)),
        ],
        compiler_params=pltpu.CompilerParams(
            collective_id=0, has_side_effects=True, vmem_limit_bytes=40 * 1024 * 1024
        ),
    )(pltpu.with_memory_space_constraint(gradients, pltpu.HBM))
    return pl.pallas_call(
        functools.partial(finish, n_groups),
        out_shape=(
            jax.ShapeDtypeStruct(gradients.shape, BF16),
            jax.ShapeDtypeStruct((n_groups, mats), F32),
            jax.ShapeDtypeStruct((1, 1), F32),
        ),
        in_specs=[vmem, vmem, vmem],
        out_specs=(any_space, vmem, vmem),
        scratch_shapes=[dma((mats,))],
        compiler_params=pltpu.CompilerParams(vmem_limit_bytes=4 * 1024 * 1024),
    )(moved, whole, owners)


def solution(mesh):
    placed = (P("expert", None, "dp", None), P("expert", None))
    return jax.shard_map(
        body,
        mesh=mesh,
        in_specs=placed,
        out_specs=(P("expert", None, "dp", None), P(), P("expert", "dp")),
        check_vma=False,
    )
```

```python
import functools
import math

import jax
import jax.numpy as jnp
from jax import lax
from jax.experimental import pallas as pl
from jax.experimental.pallas import tpu as pltpu
from jax.sharding import PartitionSpec as P

COEF_A = 3.4445
COEF_B = -4.775
COEF_C = 2.0315

RING = 4
BLK = 256
STAGES = (
    ((0, 0), (1, 0), (1, 1)),
    ((2, 0), (2, 1), (2, 2)),
    ((3, 0), (3, 1), (3, 2), (3, 3)),
)
COLUMNS = ((0, 2 * BLK), (2 * BLK, BLK), (3 * BLK, BLK))

F32 = jnp.float32
BF16 = jnp.bfloat16


def dot(a, b):
    return lax.dot_general(a, b, (((1,), (0,)), ((), ())), preferred_element_type=F32)


def dot_t(a, b):
    return lax.dot_general(a, b, (((0,), (0,)), ((), ())), preferred_element_type=F32)


def kernel(
    total_rows,
    n_groups,
    g_ref,
    u_ref,
    whole_ref,
    x_ref,
    piece_refs,
    got_refs,
    all_refs,
    tr_ref,
    s_ref,
    e1_ref,
    r_ref,
    a1_ref,
    e2_ref,
    e_ref,
    y_ref,
    rms_ref,
    tab_ref,
    go_sem,
    local_sem,
    in_send,
    in_recv,
    rs_send,
    rs_recv,
    ag_send,
    ag_recv,
    tr_send,
    tr_recv,
    out_send,
    out_recv,
    rms_send,
    rms_recv,
    tab_send,
    tab_recv,
):
    rows = g_ref.shape[2]
    cols = g_ref.shape[3]
    d = lax.axis_index("dp")
    group = lax.axis_index("expert")
    c = lax.rem(d, 2)
    x = lax.rem(d // 2, RING)
    y = d // (2 * RING)
    p = jnp.where(c == 0, x, y)
    q = jnp.where(c == 0, y, x)
    p_stride = jnp.where(c == 0, 2, 2 * RING)
    q_stride = jnp.where(c == 0, 2 * RING, 2)
    chip = d - c
    mine = c * RING + p

    def along_p(offset, core):
        return chip + (lax.rem(p + offset, RING) - p) * p_stride + core

    def along_q(offset, core):
        return chip + (lax.rem(q + offset, RING) - q) * q_stride + core

    def remote(src, dst, send, recv, dp, to_group=group):
        return pltpu.make_async_remote_copy(
            src_ref=src,
            dst_ref=dst,
            send_sem=send,
            recv_sem=recv,
            device_id=(dp, to_group),
            device_id_type=pl.DeviceIdType.MESH,
        )

    barrier = pltpu.get_barrier_semaphore()

    def greet(sem, dp, to_group=group):
        pl.semaphore_signal(
            sem, inc=1, device_id=(dp, to_group), device_id_type=pl.DeviceIdType.MESH
        )

    for offset in range(1, RING):
        greet(barrier, along_p(offset, 0))
        greet(barrier, along_q(offset, 0))

    own = pltpu.make_async_copy(
        g_ref.at[0, mine], x_ref.at[pl.ds(pl.multiple_of(c * rows, 16), rows)], local_sem.at[0]
    )
    own.start()

    @pl.when(c == 0)
    def _():
        pl.semaphore_wait(barrier, 4 * (RING - 1) + 1)
        greet(go_sem, d + 1)

    @pl.when(c == 1)
    def _():
        greet(barrier, d - 1)
        pl.semaphore_wait(go_sem, 1)

    parts = [pl.ds(*part) for part in COLUMNS]

    def slot(offset, core, part):
        return x_ref.at[pl.ds(pl.multiple_of((2 * offset + core) * rows, 16), rows), part]

    sent = []
    for number, part in enumerate(parts):
        for offset in (2, 1, 3, 0):
            back = (RING - offset) % RING
            if offset:
                copy = remote(
                    g_ref.at[0, c * RING + lax.rem(p + back, RING), :, part],
                    slot(offset, c, part),
                    in_send.at[number, 2 * offset],
                    in_recv.at[number, 2 * offset + c],
                    along_p(back, c),
                )
                copy.start()
                sent.append(copy)
            copy = remote(
                g_ref.at[0, (1 - c) * RING + lax.rem(q + back, RING), :, part],
                slot(offset, c, part),
                in_send.at[number, 2 * offset + 1],
                in_recv.at[number, 2 * offset + c],
                along_q(back, 1 - c),
            )
            copy.start()
            sent.append(copy)

    @pl.when(c == 1)
    def _():
        for offset in range(1, n_groups):
            greet(barrier, d, lax.rem(group + offset, n_groups))

    def arrive(number):
        part = parts[number]
        for offset, core in ((0, 1 - c), (1, 0), (1, 1), (3, 0), (3, 1), (2, 0), (2, 1)):
            remote(
                g_ref.at[0, 0, :, part],
                slot(offset, core, part),
                in_send.at[number, 0],
                in_recv.at[number, 2 * offset + core],
                d,
            ).wait_recv()

    diag = lax.broadcasted_iota(jnp.int32, (BLK, BLK), 0) == lax.broadcasted_iota(
        jnp.int32, (BLK, BLK), 1
    )

    def on_diag(value):
        return jnp.sum(jnp.where(diag, value, 0.0), axis=0, keepdims=True)

    def partial_gram(number):
        total = jnp.zeros((1, BLK), F32)
        for i in sorted({i for i, _ in STAGES[number]}):
            value = dot_t(x_ref[:, pl.ds(i * BLK, BLK)], x_ref[:, pl.ds(0, (i + 1) * BLK)])
            total += on_diag(value[:, i * BLK :])
            for j in range(i + 1):
                place = STAGES[number].index((i, j)) * BLK
                piece_refs[number][pl.ds(place, BLK)] = value[:, j * BLK : (j + 1) * BLK].astype(
                    BF16
                )
        return total

    def quarter(number, k):
        share = len(STAGES[number]) * BLK // RING
        return pl.ds(pl.multiple_of(k * share, share), share)

    def scatter(number):
        for offset in (2, 1, 3):
            copy = remote(
                piece_refs[number].at[quarter(number, lax.rem(q + offset, RING))],
                got_refs[number].at[RING - 1 - offset],
                rs_send.at[number, offset - 1],
                rs_recv.at[number, RING - 1 - offset],
                along_q(offset, c),
            )
            copy.start()
            sent.append(copy)

    def add_up(number):
        got_ref = got_refs[number]
        here = quarter(number, q)
        for index in range(RING - 1):
            remote(
                got_ref.at[index],
                got_ref.at[index],
                rs_send.at[number, 0],
                rs_recv.at[number, index],
                d,
            ).wait_recv()
        all_refs[number][here] = (
            (piece_refs[number][here].astype(F32) + got_ref[0].astype(F32))
            + (got_ref[1].astype(F32) + got_ref[2].astype(F32))
        ).astype(BF16)
        for offset in (2, 1, 3):
            copy = remote(
                all_refs[number].at[here],
                all_refs[number].at[here],
                ag_send.at[number, offset - 1],
                ag_recv.at[number, q],
                along_q(offset, c),
            )
            copy.start()
            sent.append(copy)

    def collect(number):
        for offset in (1, 3, 2):
            k = lax.rem(q + offset, RING)
            part = all_refs[number].at[quarter(number, k)]
            remote(part, part, ag_send.at[number, 0], ag_recv.at[number, k], d).wait_recv()

    own.wait()
    total = jnp.zeros((1, BLK), F32)
    for number in range(len(STAGES)):
        arrive(number)
        total += partial_gram(number)
        scatter(number)
    tr_ref[q] = jnp.broadcast_to(jnp.sum(total, axis=1, keepdims=True), (8, 128))
    for offset in (2, 1, 3):
        copy = remote(
            tr_ref.at[q], tr_ref.at[q], tr_send.at[offset - 1], tr_recv.at[q], along_q(offset, c)
        )
        copy.start()
        sent.append(copy)
    for number in range(len(STAGES)):
        add_up(number)

    for offset in (1, 3, 2):
        k = lax.rem(q + offset, RING)
        remote(tr_ref.at[k], tr_ref.at[k], tr_send.at[0], tr_recv.at[k], d).wait_recv()
    trace = ((tr_ref[0] + tr_ref[1]) + (tr_ref[2] + tr_ref[3]))[0:1, 0:1]
    scale = 1.0 / jnp.sqrt(trace + 1e-06)
    rms = jnp.sqrt(trace / (total_rows * cols))
    rms_ref[mine] = jnp.broadcast_to(rms, (8, 128))
    number = 0
    for offset in range(RING):
        for core in (c, 1 - c):
            if offset == 0 and core is c:
                continue
            copy = remote(
                rms_ref.at[mine],
                rms_ref.at[mine],
                rms_send.at[number],
                rms_recv.at[mine],
                along_p(offset, core),
            )
            copy.start()
            sent.append(copy)
            number += 1

    square = scale * scale

    def block(i):
        return pl.ds(i * BLK, BLK)

    def unpack(number):
        collect(number)
        for place, (i, j) in enumerate(STAGES[number]):
            one = (all_refs[number][block(place)].astype(F32) * square).astype(BF16)
            s_ref[block(i), block(j)] = one
            if i != j:
                s_ref[block(j), block(i)] = one.T

    unpack(0)
    unpack(1)

    for offset in range(1, RING):
        other = c * RING + lax.rem(p + offset, RING)
        remote(rms_ref.at[other], rms_ref.at[other], rms_send.at[0], rms_recv.at[other], d).wait_recv()
    for index in range(RING):
        other = (1 - c) * RING + index
        remote(rms_ref.at[other], rms_ref.at[other], rms_send.at[0], rms_recv.at[other], d).wait_recv()
    lane = lax.broadcasted_iota(jnp.int32, (8, 128), 1)
    line = jnp.zeros((8, 128), F32)
    for index in range(2 * RING):
        line = jnp.where(lane == index, rms_ref[index], line)
    tab_ref[group] = line
    def tell(offset, core):
        return remote(
            tab_ref.at[group],
            tab_ref.at[group],
            tab_send.at[2 * offset - 2 + core],
            tab_recv.at[group],
            chip + core,
            lax.rem(group + offset, n_groups),
        )

    @pl.when(c == 1)
    def _():
        pl.semaphore_wait(barrier, n_groups - 1)
        for offset in range(1, n_groups):
            for core in (0, 1):
                tell(offset, core).start()

    unpack(2)

    def product(out_ref, left, right, plus, by, times):
        for i in range(RING):
            wide = pl.ds(0, (i + 1) * BLK)
            value = by * plus[block(i), wide].astype(F32) + times * dot(
                left[block(i), :], right[:, wide]
            )
            value = value.astype(BF16)
            out_ref[block(i), wide] = value
            for j in range(i):
                out_ref[block(j), block(i)] = value[:, j * BLK : (j + 1) * BLK].T

    product(e1_ref, s_ref, s_ref, s_ref, COEF_B, COEF_C)

    product(r_ref, e1_ref, s_ref, s_ref, COEF_A, 1.0)
    product(a1_ref, e1_ref, r_ref, r_ref, COEF_A, 1.0)
    product(e2_ref, a1_ref, a1_ref, a1_ref, COEF_B, COEF_C)

    factor = math.sqrt(total_rows) * scale
    for n in range(RING):
        both = e1_ref[:, block(n)].astype(F32) + e2_ref[:, block(n)].astype(F32)
        e_ref[:, block(n)] = (COEF_A * both + dot(e1_ref[...], e2_ref[:, block(n)])).astype(BF16)
        value = COEF_A * COEF_A * x_ref[:, block(n)].astype(F32) + dot(
            x_ref[...], e_ref[:, block(n)]
        )
        y_ref[:, block(n)] = (factor * value).astype(BF16)

        def home(offset, core):
            return y_ref.at[
                pl.ds(pl.multiple_of((2 * offset + core) * rows, 16), rows), block(n)
            ]

        for offset, core in ((2, 0), (2, 1), (1, 0), (1, 1), (3, 0), (3, 1), (0, 1 - c)):
            remote(
                home(offset, core),
                u_ref.at[mine, :, block(n)],
                out_send.at[2 * offset + core],
                out_recv.at[mine],
                along_p(offset, core),
            ).start()
        pltpu.make_async_copy(home(0, c), u_ref.at[mine, :, block(n)], local_sem.at[1]).start()

    for offset in range(1, n_groups):
        other = lax.rem(group + offset, n_groups)
        remote(
            tab_ref.at[other], tab_ref.at[other], tab_send.at[0], tab_recv.at[other], d
        ).wait_recv()
    sub = lax.broadcasted_iota(jnp.int32, (8, 128), 0)
    whole = jnp.zeros((8, 128), F32)
    for index in range(n_groups):
        whole = jnp.where(sub == index, tab_ref[index], whole)
    whole_ref[...] = whole

    def all_columns(other, offset, core):
        return remote(
            y_ref.at[pl.ds(pl.multiple_of((2 * offset + core) * rows, 16), rows)],
            u_ref.at[other],
            out_send.at[2 * offset + core],
            out_recv.at[other],
            d,
        )

    pltpu.make_async_copy(y_ref.at[pl.ds(0, rows)], u_ref.at[mine], local_sem.at[1]).wait()
    for offset in range(1, RING):
        all_columns(c * RING + lax.rem(p + offset, RING), 0, 0).wait_recv()
    for index in range(RING):
        all_columns((1 - c) * RING + index, 0, 0).wait_recv()
    for offset, core in ((2, 0), (2, 1), (1, 0), (1, 1), (3, 0), (3, 1), (0, 1 - c)):
        all_columns(mine, offset, core).wait_send()
    for copy in sent:
        copy.wait_send()

    @pl.when(c == 1)
    def _():
        for offset in range(1, n_groups):
            for core in (0, 1):
                tell(offset, core).wait_send()


def finish(n_groups, u_ref, whole_ref, owners_ref, update_ref, table_ref, owned_ref, sem):
    mats = u_ref.shape[0]
    copies = [
        pltpu.make_async_copy(u_ref.at[m], update_ref.at[0, m], sem.at[m]) for m in range(mats)
    ]
    for copy in copies:
        copy.start()
    table = whole_ref[...][0:n_groups, 0:mats]
    table_ref[...] = table
    sub = lax.broadcasted_iota(jnp.int32, table.shape, 0)
    mask = (sub == lax.axis_index("expert")) & (owners_ref[...] == lax.axis_index("dp") // 4)
    hit = jnp.sum(jnp.where(mask, table, 0.0), axis=0, keepdims=True)
    owned_ref[...] = jnp.sum(hit, axis=1, keepdims=True)
    for copy in copies:
        copy.wait()


def body(gradients, owners):
    _, mats, rows, cols = gradients.shape
    n_groups = lax.axis_size("expert")
    total_rows = rows * lax.axis_size("dp")
    any_space = pl.BlockSpec(memory_space=pl.ANY)
    vmem = pl.BlockSpec(memory_space=pltpu.VMEM)
    full = pltpu.VMEM((cols, cols), BF16)
    dma = pltpu.SemaphoreType.DMA
    stacks = [len(stage) * BLK for stage in STAGES]
    moved, whole = pl.pallas_call(
        functools.partial(kernel, total_rows, n_groups),
        out_shape=(
            pltpu.VMEM((mats, rows, cols), BF16),
            jax.ShapeDtypeStruct((8, 128), F32),
        ),
        in_specs=[any_space],
        out_specs=(vmem, vmem),
        scratch_shapes=[
            pltpu.VMEM((mats * rows, cols), BF16),
            tuple(pltpu.VMEM((stack, BLK), BF16) for stack in stacks),
            tuple(pltpu.VMEM((RING - 1, stack // RING, BLK), BF16) for stack in stacks),
            tuple(pltpu.VMEM((stack, BLK), BF16) for stack in stacks),
            pltpu.VMEM((RING, 8, 128), F32),
            full,
            full,
            full,
            full,
            full,
            full,
            pltpu.VMEM((mats * rows, cols), BF16),
            pltpu.VMEM((2 * RING, 8, 128), F32),
            pltpu.VMEM((n_groups, 8, 128), F32),
            pltpu.SemaphoreType.REGULAR,
            dma((2,)),
            dma((len(STAGES), 2 * RING)),
            dma((len(STAGES), 2 * RING)),
            dma((len(STAGES), RING - 1)),
            dma((len(STAGES), RING - 1)),
            dma((len(STAGES), RING - 1)),
            dma((len(STAGES), RING)),
            dma((RING - 1,)),
            dma((RING,)),
            dma((2 * RING,)),
            dma((2 * RING,)),
            dma((2 * RING - 1,)),
            dma((2 * RING,)),
            dma((2 * (n_groups - 1),)),
            dma((n_groups,)),
        ],
        compiler_params=pltpu.CompilerParams(
            collective_id=0, has_side_effects=True, vmem_limit_bytes=40 * 1024 * 1024
        ),
    )(pltpu.with_memory_space_constraint(gradients, pltpu.HBM))
    return pl.pallas_call(
        functools.partial(finish, n_groups),
        out_shape=(
            jax.ShapeDtypeStruct(gradients.shape, BF16),
            jax.ShapeDtypeStruct((n_groups, mats), F32),
            jax.ShapeDtypeStruct((1, 1), F32),
        ),
        in_specs=[vmem, vmem, vmem],
        out_specs=(any_space, vmem, vmem),
        scratch_shapes=[dma((mats,))],
        compiler_params=pltpu.CompilerParams(vmem_limit_bytes=4 * 1024 * 1024),
    )(moved, whole, owners)


def solution(mesh):
    placed = (P("expert", None, "dp", None), P("expert", None))
    return jax.shard_map(
        body,
        mesh=mesh,
        in_specs=placed,
        out_specs=(P("expert", None, "dp", None), P(), P("expert", "dp")),
        check_vma=False,
    )
```

```python
import functools
import math

import jax
import jax.numpy as jnp
from jax import lax
from jax.experimental import pallas as pl
from jax.experimental.pallas import tpu as pltpu
from jax.sharding import PartitionSpec as P

COEF_A = 3.4445
COEF_B = -4.775
COEF_C = 2.0315

RING = 4
BLK = 256
TILE = 128
STAGES = (((0, BLK), (BLK, BLK)), ((2 * BLK, BLK),), ((3 * BLK, TILE),), ((3 * BLK + TILE, TILE),))
FIRST_STAGES = len([stage for stage in STAGES if sum(stage[-1]) <= 3 * BLK])


def tiles(stage):
    first = stage[0][0] // TILE
    last = sum(stage[-1]) // TILE
    return [(i, j) for i in range(first, last) for j in range(i + 1)]


F32 = jnp.float32
BF16 = jnp.bfloat16


def dot(a, b):
    return lax.dot_general(a, b, (((1,), (0,)), ((), ())), preferred_element_type=F32)


def dot_t(a, b):
    return lax.dot_general(a, b, (((0,), (0,)), ((), ())), preferred_element_type=F32)


def kernel(
    total_rows,
    n_groups,
    g_ref,
    u_ref,
    whole_ref,
    x_ref,
    piece_refs,
    got_refs,
    all_refs,
    tr_ref,
    s_ref,
    t_ref,
    e1_ref,
    r_ref,
    a1_ref,
    e2_ref,
    e_ref,
    y_ref,
    rms_ref,
    tab_ref,
    go_sem,
    local_sem,
    in_send,
    in_recv,
    rs_send,
    rs_recv,
    ag_send,
    ag_recv,
    tr_send,
    tr_recv,
    out_send,
    out_recv,
    rms_send,
    rms_recv,
    tab_send,
    tab_recv,
):
    rows = g_ref.shape[2]
    cols = g_ref.shape[3]
    d = lax.axis_index("dp")
    group = lax.axis_index("expert")
    c = lax.rem(d, 2)
    x = lax.rem(d // 2, RING)
    y = d // (2 * RING)
    p = jnp.where(c == 0, x, y)
    q = jnp.where(c == 0, y, x)
    p_stride = jnp.where(c == 0, 2, 2 * RING)
    q_stride = jnp.where(c == 0, 2 * RING, 2)
    chip = d - c
    mine = c * RING + p

    def along_p(offset, core):
        return chip + (lax.rem(p + offset, RING) - p) * p_stride + core

    def along_q(offset, core):
        return chip + (lax.rem(q + offset, RING) - q) * q_stride + core

    def remote(src, dst, send, recv, dp, to_group=group):
        return pltpu.make_async_remote_copy(
            src_ref=src,
            dst_ref=dst,
            send_sem=send,
            recv_sem=recv,
            device_id=(dp, to_group),
            device_id_type=pl.DeviceIdType.MESH,
        )

    barrier = pltpu.get_barrier_semaphore()

    def greet(sem, dp, to_group=group):
        pl.semaphore_signal(
            sem, inc=1, device_id=(dp, to_group), device_id_type=pl.DeviceIdType.MESH
        )

    for offset in range(1, RING):
        greet(barrier, along_p(offset, 0))
        greet(barrier, along_q(offset, 0))

    own = pltpu.make_async_copy(
        g_ref.at[0, mine], x_ref.at[pl.ds(pl.multiple_of(c * rows, 16), rows)], local_sem.at[0]
    )
    own.start()

    @pl.when(c == 0)
    def _():
        pl.semaphore_wait(barrier, 4 * (RING - 1) + 1)
        greet(go_sem, d + 1)

    @pl.when(c == 1)
    def _():
        greet(barrier, d - 1)
        pl.semaphore_wait(go_sem, 1)

    parts = [pl.ds(stage[0][0], sum(stage[-1]) - stage[0][0]) for stage in STAGES]

    def slot(offset, core, part):
        return x_ref.at[pl.ds(pl.multiple_of((2 * offset + core) * rows, 16), rows), part]

    sent = []
    for number, part in enumerate(parts):
        for offset in (2, 1, 3, 0):
            back = (RING - offset) % RING
            if offset:
                copy = remote(
                    g_ref.at[0, c * RING + lax.rem(p + back, RING), :, part],
                    slot(offset, c, part),
                    in_send.at[number, 2 * offset],
                    in_recv.at[number, 2 * offset + c],
                    along_p(back, c),
                )
                copy.start()
                sent.append(copy)
            copy = remote(
                g_ref.at[0, (1 - c) * RING + lax.rem(q + back, RING), :, part],
                slot(offset, c, part),
                in_send.at[number, 2 * offset + 1],
                in_recv.at[number, 2 * offset + c],
                along_q(back, 1 - c),
            )
            copy.start()
            sent.append(copy)

    @pl.when(c == 1)
    def _():
        for offset in range(1, n_groups):
            greet(barrier, d, lax.rem(group + offset, n_groups))

    def arrive(number):
        part = parts[number]
        for offset, core in ((0, 1 - c), (1, 0), (1, 1), (3, 0), (3, 1), (2, 0), (2, 1)):
            remote(
                g_ref.at[0, 0, :, part],
                slot(offset, core, part),
                in_send.at[number, 0],
                in_recv.at[number, 2 * offset + core],
                d,
            ).wait_recv()

    def partial_gram(number):
        total = jnp.zeros((1, 1), F32)
        places = tiles(STAGES[number])
        for first, count in STAGES[number]:
            value = dot_t(x_ref[:, pl.ds(first, count)], x_ref[:, pl.ds(0, first + count)])
            diag = lax.broadcasted_iota(jnp.int32, (count, count), 0) == lax.broadcasted_iota(
                jnp.int32, (count, count), 1
            )
            line = jnp.sum(jnp.where(diag, value[:, first:], 0.0), axis=0, keepdims=True)
            total += jnp.sum(line, axis=1, keepdims=True)
            for down in range(0, count, TILE):
                i = (first + down) // TILE
                for j in range(i + 1):
                    piece_refs[number][pl.ds(places.index((i, j)) * TILE, TILE)] = value[
                        down : down + TILE, j * TILE : (j + 1) * TILE
                    ].astype(BF16)
        return total

    def quarter(number, k):
        share = len(tiles(STAGES[number])) * TILE // RING
        return pl.ds(pl.multiple_of(k * share, share), share)

    def scatter(number):
        for offset in (2, 1, 3):
            copy = remote(
                piece_refs[number].at[quarter(number, lax.rem(q + offset, RING))],
                got_refs[number].at[RING - 1 - offset],
                rs_send.at[number, offset - 1],
                rs_recv.at[number, RING - 1 - offset],
                along_q(offset, c),
            )
            copy.start()
            sent.append(copy)

    def add_up(number):
        got_ref = got_refs[number]
        here = quarter(number, q)
        for index in range(RING - 1):
            remote(
                got_ref.at[index],
                got_ref.at[index],
                rs_send.at[number, 0],
                rs_recv.at[number, index],
                d,
            ).wait_recv()
        all_refs[number][here] = (
            (piece_refs[number][here].astype(F32) + got_ref[0].astype(F32))
            + (got_ref[1].astype(F32) + got_ref[2].astype(F32))
        ).astype(BF16)
        for offset in (2, 1, 3):
            copy = remote(
                all_refs[number].at[here],
                all_refs[number].at[here],
                ag_send.at[number, offset - 1],
                ag_recv.at[number, q],
                along_q(offset, c),
            )
            copy.start()
            sent.append(copy)

    def collect(number):
        for offset in (1, 3, 2):
            k = lax.rem(q + offset, RING)
            part = all_refs[number].at[quarter(number, k)]
            remote(part, part, ag_send.at[number, 0], ag_recv.at[number, k], d).wait_recv()

    own.wait()
    total = jnp.zeros((1, 1), F32)
    for number in range(len(STAGES)):
        arrive(number)
        total += partial_gram(number)
        scatter(number)
    tr_ref[q] = jnp.broadcast_to(total, (8, 128))
    for offset in (2, 1, 3):
        copy = remote(
            tr_ref.at[q], tr_ref.at[q], tr_send.at[offset - 1], tr_recv.at[q], along_q(offset, c)
        )
        copy.start()
        sent.append(copy)
    for number in range(len(STAGES)):
        add_up(number)

    for offset in (1, 3, 2):
        k = lax.rem(q + offset, RING)
        remote(tr_ref.at[k], tr_ref.at[k], tr_send.at[0], tr_recv.at[k], d).wait_recv()
    trace = ((tr_ref[0] + tr_ref[1]) + (tr_ref[2] + tr_ref[3]))[0:1, 0:1]
    scale = 1.0 / jnp.sqrt(trace + 1e-06)
    rms = jnp.sqrt(trace / (total_rows * cols))
    rms_ref[mine] = jnp.broadcast_to(rms, (8, 128))
    number = 0
    for offset in range(RING):
        for core in (c, 1 - c):
            if offset == 0 and core is c:
                continue
            copy = remote(
                rms_ref.at[mine],
                rms_ref.at[mine],
                rms_send.at[number],
                rms_recv.at[mine],
                along_p(offset, core),
            )
            copy.start()
            sent.append(copy)
            number += 1

    square = scale * scale

    def block(i):
        return pl.ds(i * BLK, BLK)

    def unpack(number):
        collect(number)
        for place, (i, j) in enumerate(tiles(STAGES[number])):
            down, right = pl.ds(i * TILE, TILE), pl.ds(j * TILE, TILE)
            one = all_refs[number][pl.ds(place * TILE, TILE)].astype(F32) * square
            one = one.astype(BF16)
            s_ref[down, right] = one
            if i != j:
                s_ref[right, down] = one.T

    for number in range(FIRST_STAGES):
        unpack(number)

    for offset in range(1, RING):
        other = c * RING + lax.rem(p + offset, RING)
        remote(rms_ref.at[other], rms_ref.at[other], rms_send.at[0], rms_recv.at[other], d).wait_recv()
    for index in range(RING):
        other = (1 - c) * RING + index
        remote(rms_ref.at[other], rms_ref.at[other], rms_send.at[0], rms_recv.at[other], d).wait_recv()
    lane = lax.broadcasted_iota(jnp.int32, (8, 128), 1)
    line = jnp.zeros((8, 128), F32)
    for index in range(2 * RING):
        line = jnp.where(lane == index, rms_ref[index], line)
    tab_ref[group] = line
    def tell(offset, core):
        return remote(
            tab_ref.at[group],
            tab_ref.at[group],
            tab_send.at[2 * offset - 2 + core],
            tab_recv.at[group],
            chip + core,
            lax.rem(group + offset, n_groups),
        )

    @pl.when(c == 1)
    def _():
        pl.semaphore_wait(barrier, n_groups - 1)
        for offset in range(1, n_groups):
            for core in (0, 1):
                tell(offset, core).start()

    early = 3 * BLK
    for i in range(RING - 1):
        wide = pl.ds(0, (i + 1) * BLK)
        t_ref[block(i), wide] = COEF_B * s_ref[block(i), wide].astype(F32) + COEF_C * dot(
            s_ref[block(i), pl.ds(0, early)], s_ref[pl.ds(0, early), wide]
        )
    for number in range(FIRST_STAGES, len(STAGES)):
        unpack(number)

    def turn_over(out_ref, i, value):
        value = value.astype(BF16)
        out_ref[block(i), pl.ds(0, (i + 1) * BLK)] = value
        for j in range(i):
            out_ref[block(j), block(i)] = value[:, j * BLK : (j + 1) * BLK].T

    def product(out_ref, left, right, plus, by, times, first=0):
        for i in range(first, RING):
            wide = pl.ds(0, (i + 1) * BLK)
            value = by * plus[block(i), wide].astype(F32) + times * dot(
                left[block(i), :], right[:, wide]
            )
            turn_over(out_ref, i, value)

    for i in range(RING - 1):
        wide = pl.ds(0, (i + 1) * BLK)
        value = t_ref[block(i), wide] + COEF_C * dot(s_ref[block(i), block(3)], s_ref[block(3), wide])
        turn_over(e1_ref, i, value)
    product(e1_ref, s_ref, s_ref, s_ref, COEF_B, COEF_C, RING - 1)

    product(r_ref, e1_ref, s_ref, s_ref, COEF_A, 1.0)
    product(a1_ref, e1_ref, r_ref, r_ref, COEF_A, 1.0)
    def column(out_ref, left, right, plus, by, times, n):
        down = pl.ds(n * BLK, cols - n * BLK)
        value = by * plus(down, block(n)) + times * dot(left[down, :], right[:, block(n)])
        value = value.astype(BF16)
        out_ref[down, block(n)] = value
        for i in range(n + 1, RING):
            out_ref[block(n), block(i)] = value[(i - n) * BLK : (i - n + 1) * BLK, :].T

    def second(n):
        def plus(down, right):
            return a1_ref[down, right].astype(F32)

        column(e2_ref, a1_ref, a1_ref, plus, COEF_B, COEF_C, n)


    factor = math.sqrt(total_rows) * scale
    for n in range(RING):
        if n < 2:
            for later in range(n, RING if n else 1):
                second(later)

        def plus(down, right):
            return e1_ref[down, right].astype(F32) + e2_ref[down, right].astype(F32)

        column(e_ref, e1_ref, e2_ref, plus, COEF_A, 1.0, n)

        def update(span):
            value = COEF_A * COEF_A * x_ref[span, block(n)].astype(F32) + dot(
                x_ref[span, :], e_ref[:, block(n)]
            )
            y_ref[span, block(n)] = (factor * value).astype(BF16)

        def home(offset, core):
            return y_ref.at[
                pl.ds(pl.multiple_of((2 * offset + core) * rows, 16), rows), block(n)
            ]

        def back(offset, core):
            remote(
                home(offset, core),
                u_ref.at[mine, :, block(n)],
                out_send.at[2 * offset + core],
                out_recv.at[mine],
                along_p(offset, core),
            ).start()

        if n:
            update(pl.ds(0, 2 * RING * rows))
        for offset in (2, 1, 3, 0):
            if n == 0:
                update(pl.ds(2 * offset * rows, 2 * rows))
            if offset:
                back(offset, 0)
                back(offset, 1)
            else:
                back(0, 1 - c)
                pltpu.make_async_copy(home(0, c), u_ref.at[mine, :, block(n)], local_sem.at[1]).start()

    for offset in range(1, n_groups):
        other = lax.rem(group + offset, n_groups)
        remote(
            tab_ref.at[other], tab_ref.at[other], tab_send.at[0], tab_recv.at[other], d
        ).wait_recv()
    sub = lax.broadcasted_iota(jnp.int32, (8, 128), 0)
    whole = jnp.zeros((8, 128), F32)
    for index in range(n_groups):
        whole = jnp.where(sub == index, tab_ref[index], whole)
    whole_ref[...] = whole

    def all_columns(other, offset, core):
        return remote(
            y_ref.at[pl.ds(pl.multiple_of((2 * offset + core) * rows, 16), rows)],
            u_ref.at[other],
            out_send.at[2 * offset + core],
            out_recv.at[other],
            d,
        )

    pltpu.make_async_copy(y_ref.at[pl.ds(0, rows)], u_ref.at[mine], local_sem.at[1]).wait()
    for offset in range(1, RING):
        all_columns(c * RING + lax.rem(p + offset, RING), 0, 0).wait_recv()
    for index in range(RING):
        all_columns((1 - c) * RING + index, 0, 0).wait_recv()
    for offset, core in ((2, 0), (2, 1), (1, 0), (1, 1), (3, 0), (3, 1), (0, 1 - c)):
        all_columns(mine, offset, core).wait_send()
    for copy in sent:
        copy.wait_send()

    @pl.when(c == 1)
    def _():
        for offset in range(1, n_groups):
            for core in (0, 1):
                tell(offset, core).wait_send()


def finish(n_groups, u_ref, whole_ref, owners_ref, update_ref, table_ref, owned_ref, sem):
    mats = u_ref.shape[0]
    copies = [
        pltpu.make_async_copy(u_ref.at[m], update_ref.at[0, m], sem.at[m]) for m in range(mats)
    ]
    for copy in copies:
        copy.start()
    table = whole_ref[...][0:n_groups, 0:mats]
    table_ref[...] = table
    sub = lax.broadcasted_iota(jnp.int32, table.shape, 0)
    mask = (sub == lax.axis_index("expert")) & (owners_ref[...] == lax.axis_index("dp") // 4)
    hit = jnp.sum(jnp.where(mask, table, 0.0), axis=0, keepdims=True)
    owned_ref[...] = jnp.sum(hit, axis=1, keepdims=True)
    for copy in copies:
        copy.wait()


def body(gradients, owners):
    _, mats, rows, cols = gradients.shape
    n_groups = lax.axis_size("expert")
    total_rows = rows * lax.axis_size("dp")
    any_space = pl.BlockSpec(memory_space=pl.ANY)
    vmem = pl.BlockSpec(memory_space=pltpu.VMEM)
    full = pltpu.VMEM((cols, cols), BF16)
    dma = pltpu.SemaphoreType.DMA
    stacks = [len(tiles(stage)) * TILE for stage in STAGES]
    moved, whole = pl.pallas_call(
        functools.partial(kernel, total_rows, n_groups),
        out_shape=(
            pltpu.VMEM((mats, rows, cols), BF16),
            jax.ShapeDtypeStruct((8, 128), F32),
        ),
        in_specs=[any_space],
        out_specs=(vmem, vmem),
        scratch_shapes=[
            pltpu.VMEM((mats * rows, cols), BF16),
            tuple(pltpu.VMEM((stack, TILE), BF16) for stack in stacks),
            tuple(pltpu.VMEM((RING - 1, stack // RING, TILE), BF16) for stack in stacks),
            tuple(pltpu.VMEM((stack, TILE), BF16) for stack in stacks),
            pltpu.VMEM((RING, 8, 128), F32),
            full,
            pltpu.VMEM((3 * BLK, 3 * BLK), F32),
            full,
            full,
            full,
            full,
            full,
            pltpu.VMEM((mats * rows, cols), BF16),
            pltpu.VMEM((2 * RING, 8, 128), F32),
            pltpu.VMEM((n_groups, 8, 128), F32),
            pltpu.SemaphoreType.REGULAR,
            dma((2,)),
            dma((len(STAGES), 2 * RING)),
            dma((len(STAGES), 2 * RING)),
            dma((len(STAGES), RING - 1)),
            dma((len(STAGES), RING - 1)),
            dma((len(STAGES), RING - 1)),
            dma((len(STAGES), RING)),
            dma((RING - 1,)),
            dma((RING,)),
            dma((2 * RING,)),
            dma((2 * RING,)),
            dma((2 * RING - 1,)),
            dma((2 * RING,)),
            dma((2 * (n_groups - 1),)),
            dma((n_groups,)),
        ],
        compiler_params=pltpu.CompilerParams(
            collective_id=0, has_side_effects=True, vmem_limit_bytes=40 * 1024 * 1024
        ),
    )(pltpu.with_memory_space_constraint(gradients, pltpu.HBM))
    return pl.pallas_call(
        functools.partial(finish, n_groups),
        out_shape=(
            jax.ShapeDtypeStruct(gradients.shape, BF16),
            jax.ShapeDtypeStruct((n_groups, mats), F32),
            jax.ShapeDtypeStruct((1, 1), F32),
        ),
        in_specs=[vmem, vmem, vmem],
        out_specs=(any_space, vmem, vmem),
        scratch_shapes=[dma((mats,))],
        compiler_params=pltpu.CompilerParams(vmem_limit_bytes=4 * 1024 * 1024),
    )(moved, whole, owners)


def solution(mesh):
    placed = (P("expert", None, "dp", None), P("expert", None))
    return jax.shard_map(
        body,
        mesh=mesh,
        in_specs=placed,
        out_specs=(P("expert", None, "dp", None), P(), P("expert", "dp")),
        check_vma=False,
    )
```

```python
import functools
import math

import jax
import jax.numpy as jnp
from jax import lax
from jax.experimental import pallas as pl
from jax.experimental.pallas import tpu as pltpu
from jax.sharding import PartitionSpec as P

COEF_A = 3.4445
COEF_B = -4.775
COEF_C = 2.0315

RING = 4
BLK = 256
TILE = 128
STAGES = (((0, BLK), (BLK, BLK)), ((2 * BLK, BLK),), ((3 * BLK, TILE),), ((3 * BLK + TILE, TILE),))
FIRST_STAGES = len([stage for stage in STAGES if sum(stage[-1]) <= 3 * BLK])


def tiles(stage):
    first = stage[0][0] // TILE
    last = sum(stage[-1]) // TILE
    return [(i, j) for i in range(first, last) for j in range(i + 1)]


F32 = jnp.float32
BF16 = jnp.bfloat16


def dot(a, b):
    return lax.dot_general(a, b, (((1,), (0,)), ((), ())), preferred_element_type=F32)


def dot_t(a, b):
    return lax.dot_general(a, b, (((0,), (0,)), ((), ())), preferred_element_type=F32)


def kernel(
    total_rows,
    n_groups,
    g_ref,
    u_ref,
    whole_ref,
    x_ref,
    piece_refs,
    got_refs,
    all_refs,
    tr_ref,
    s_ref,
    t_ref,
    e1_ref,
    r_ref,
    a1_ref,
    e2_ref,
    e_ref,
    y_ref,
    rms_ref,
    tab_ref,
    go_sem,
    local_sem,
    in_send,
    in_recv,
    rs_send,
    rs_recv,
    ag_send,
    ag_recv,
    tr_send,
    tr_recv,
    out_send,
    out_recv,
    rms_send,
    rms_recv,
    tab_send,
    tab_recv,
):
    rows = g_ref.shape[2]
    cols = g_ref.shape[3]
    d = lax.axis_index("dp")
    group = lax.axis_index("expert")
    c = lax.rem(d, 2)
    x = lax.rem(d // 2, RING)
    y = d // (2 * RING)
    p = jnp.where(c == 0, x, y)
    q = jnp.where(c == 0, y, x)
    p_stride = jnp.where(c == 0, 2, 2 * RING)
    q_stride = jnp.where(c == 0, 2 * RING, 2)
    chip = d - c
    mine = c * RING + p

    def along_p(offset, core):
        return chip + (lax.rem(p + offset, RING) - p) * p_stride + core

    def along_q(offset, core):
        return chip + (lax.rem(q + offset, RING) - q) * q_stride + core

    def remote(src, dst, send, recv, dp, to_group=group):
        return pltpu.make_async_remote_copy(
            src_ref=src,
            dst_ref=dst,
            send_sem=send,
            recv_sem=recv,
            device_id=(dp, to_group),
            device_id_type=pl.DeviceIdType.MESH,
        )

    barrier = pltpu.get_barrier_semaphore()

    def greet(sem, dp, to_group=group):
        pl.semaphore_signal(
            sem, inc=1, device_id=(dp, to_group), device_id_type=pl.DeviceIdType.MESH
        )

    for offset in range(1, RING):
        greet(barrier, along_p(offset, 0))
        greet(barrier, along_q(offset, 0))

    own = pltpu.make_async_copy(
        g_ref.at[0, mine], x_ref.at[pl.ds(pl.multiple_of(c * rows, 16), rows)], local_sem.at[0]
    )
    own.start()

    @pl.when(c == 0)
    def _():
        pl.semaphore_wait(barrier, 4 * (RING - 1) + 1)
        greet(go_sem, d + 1)

    @pl.when(c == 1)
    def _():
        greet(barrier, d - 1)
        pl.semaphore_wait(go_sem, 1)

    parts = [pl.ds(stage[0][0], sum(stage[-1]) - stage[0][0]) for stage in STAGES]

    def slot(offset, core, part):
        return x_ref.at[pl.ds(pl.multiple_of((2 * offset + core) * rows, 16), rows), part]

    sent = []
    for number, part in enumerate(parts):
        for offset in (2, 1, 3, 0):
            back = (RING - offset) % RING
            if offset:
                copy = remote(
                    g_ref.at[0, c * RING + lax.rem(p + back, RING), :, part],
                    slot(offset, c, part),
                    in_send.at[number, 2 * offset],
                    in_recv.at[number, 2 * offset + c],
                    along_p(back, c),
                )
                copy.start()
                sent.append(copy)
            copy = remote(
                g_ref.at[0, (1 - c) * RING + lax.rem(q + back, RING), :, part],
                slot(offset, c, part),
                in_send.at[number, 2 * offset + 1],
                in_recv.at[number, 2 * offset + c],
                along_q(back, 1 - c),
            )
            copy.start()
            sent.append(copy)

    @pl.when(c == 1)
    def _():
        for offset in range(1, n_groups):
            greet(barrier, d, lax.rem(group + offset, n_groups))

    def arrive(number, offsets=(0, 1, 3, 2)):
        part = parts[number]
        slots = [(offset, core) for offset in offsets for core in (0, 1) if offset]
        if 0 in offsets:
            slots.insert(0, (0, 1 - c))
        for offset, core in slots:
            remote(
                g_ref.at[0, 0, :, part],
                slot(offset, core, part),
                in_send.at[number, 0],
                in_recv.at[number, 2 * offset + core],
                d,
            ).wait_recv()

    def partial_gram(number):
        total = jnp.zeros((1, 1), F32)
        places = tiles(STAGES[number])
        chunks = [((0, 1, 3, 2), 0, 2 * RING)]
        if number == len(STAGES) - 1:
            chunks = [((0, 1), 0, 4), ((3,), 6, 2), ((2,), 4, 2)]
        for first, count in STAGES[number]:
            value = None
            for offsets, start, size in chunks:
                if number == len(STAGES) - 1 and first == STAGES[number][0][0]:
                    arrive(number, offsets)
                here = pl.ds(start * rows, size * rows)
                term = dot_t(x_ref[here, pl.ds(first, count)], x_ref[here, pl.ds(0, first + count)])
                value = term if value is None else value + term
            diag = lax.broadcasted_iota(jnp.int32, (count, count), 0) == lax.broadcasted_iota(
                jnp.int32, (count, count), 1
            )
            line = jnp.sum(jnp.where(diag, value[:, first:], 0.0), axis=0, keepdims=True)
            total += jnp.sum(line, axis=1, keepdims=True)
            for down in range(0, count, TILE):
                i = (first + down) // TILE
                for j in range(i + 1):
                    piece_refs[number][pl.ds(places.index((i, j)) * TILE, TILE)] = value[
                        down : down + TILE, j * TILE : (j + 1) * TILE
                    ].astype(BF16)
        return total

    def quarter(number, k):
        share = len(tiles(STAGES[number])) * TILE // RING
        return pl.ds(pl.multiple_of(k * share, share), share)

    def scatter(number):
        for offset in (2, 1, 3):
            copy = remote(
                piece_refs[number].at[quarter(number, lax.rem(q + offset, RING))],
                got_refs[number].at[RING - 1 - offset],
                rs_send.at[number, offset - 1],
                rs_recv.at[number, RING - 1 - offset],
                along_q(offset, c),
            )
            copy.start()
            sent.append(copy)

    def add_up(number):
        got_ref = got_refs[number]
        here = quarter(number, q)
        for index in range(RING - 1):
            remote(
                got_ref.at[index],
                got_ref.at[index],
                rs_send.at[number, 0],
                rs_recv.at[number, index],
                d,
            ).wait_recv()
        all_refs[number][here] = (
            (piece_refs[number][here].astype(F32) + got_ref[0].astype(F32))
            + (got_ref[1].astype(F32) + got_ref[2].astype(F32))
        ).astype(BF16)
        for offset in (2, 1, 3):
            copy = remote(
                all_refs[number].at[here],
                all_refs[number].at[here],
                ag_send.at[number, offset - 1],
                ag_recv.at[number, q],
                along_q(offset, c),
            )
            copy.start()
            sent.append(copy)

    def collect(number):
        for offset in (1, 3, 2):
            k = lax.rem(q + offset, RING)
            part = all_refs[number].at[quarter(number, k)]
            remote(part, part, ag_send.at[number, 0], ag_recv.at[number, k], d).wait_recv()

    own.wait()
    total = jnp.zeros((1, 1), F32)
    for number in range(len(STAGES)):
        if number < len(STAGES) - 1:
            arrive(number)
        total += partial_gram(number)
        scatter(number)
    tr_ref[q] = jnp.broadcast_to(total, (8, 128))
    for offset in (2, 1, 3):
        copy = remote(
            tr_ref.at[q], tr_ref.at[q], tr_send.at[offset - 1], tr_recv.at[q], along_q(offset, c)
        )
        copy.start()
        sent.append(copy)
    for number in range(len(STAGES)):
        add_up(number)

    for offset in (1, 3, 2):
        k = lax.rem(q + offset, RING)
        remote(tr_ref.at[k], tr_ref.at[k], tr_send.at[0], tr_recv.at[k], d).wait_recv()
    trace = ((tr_ref[0] + tr_ref[1]) + (tr_ref[2] + tr_ref[3]))[0:1, 0:1]
    scale = 1.0 / jnp.sqrt(trace + 1e-06)
    rms = jnp.sqrt(trace / (total_rows * cols))
    rms_ref[mine] = jnp.broadcast_to(rms, (8, 128))
    number = 0
    for offset in range(RING):
        for core in (c, 1 - c):
            if offset == 0 and core is c:
                continue
            copy = remote(
                rms_ref.at[mine],
                rms_ref.at[mine],
                rms_send.at[number],
                rms_recv.at[mine],
                along_p(offset, core),
            )
            copy.start()
            sent.append(copy)
            number += 1

    square = scale * scale

    def block(i):
        return pl.ds(i * BLK, BLK)

    def unpack(number):
        collect(number)
        for place, (i, j) in enumerate(tiles(STAGES[number])):
            down, right = pl.ds(i * TILE, TILE), pl.ds(j * TILE, TILE)
            one = all_refs[number][pl.ds(place * TILE, TILE)].astype(F32) * square
            one = one.astype(BF16)
            s_ref[down, right] = one
            if i != j:
                s_ref[right, down] = one.T

    for number in range(FIRST_STAGES):
        unpack(number)

    for offset in range(1, RING):
        other = c * RING + lax.rem(p + offset, RING)
        remote(rms_ref.at[other], rms_ref.at[other], rms_send.at[0], rms_recv.at[other], d).wait_recv()
    for index in range(RING):
        other = (1 - c) * RING + index
        remote(rms_ref.at[other], rms_ref.at[other], rms_send.at[0], rms_recv.at[other], d).wait_recv()
    lane = lax.broadcasted_iota(jnp.int32, (8, 128), 1)
    line = jnp.zeros((8, 128), F32)
    for index in range(2 * RING):
        line = jnp.where(lane == index, rms_ref[index], line)
    tab_ref[group] = line
    def tell(offset, core):
        return remote(
            tab_ref.at[group],
            tab_ref.at[group],
            tab_send.at[2 * offset - 2 + core],
            tab_recv.at[group],
            chip + core,
            lax.rem(group + offset, n_groups),
        )

    @pl.when(c == 1)
    def _():
        pl.semaphore_wait(barrier, n_groups - 1)
        for offset in range(1, n_groups):
            for core in (0, 1):
                tell(offset, core).start()

    early = 3 * BLK
    for i in range(RING - 1):
        wide = pl.ds(0, (i + 1) * BLK)
        t_ref[block(i), wide] = COEF_B * s_ref[block(i), wide].astype(F32) + COEF_C * dot(
            s_ref[block(i), pl.ds(0, early)], s_ref[pl.ds(0, early), wide]
        )
    for number in range(FIRST_STAGES, len(STAGES)):
        unpack(number)

    def turn_over(out_ref, i, value):
        value = value.astype(BF16)
        out_ref[block(i), pl.ds(0, (i + 1) * BLK)] = value
        for j in range(i):
            out_ref[block(j), block(i)] = value[:, j * BLK : (j + 1) * BLK].T

    def product(out_ref, left, right, plus, by, times, first=0):
        for i in range(first, RING):
            wide = pl.ds(0, (i + 1) * BLK)
            value = by * plus[block(i), wide].astype(F32) + times * dot(
                left[block(i), :], right[:, wide]
            )
            turn_over(out_ref, i, value)

    for i in range(RING - 1):
        wide = pl.ds(0, (i + 1) * BLK)
        value = t_ref[block(i), wide] + COEF_C * dot(s_ref[block(i), block(3)], s_ref[block(3), wide])
        turn_over(e1_ref, i, value)
    product(e1_ref, s_ref, s_ref, s_ref, COEF_B, COEF_C, RING - 1)

    product(r_ref, e1_ref, s_ref, s_ref, COEF_A, 1.0)
    product(a1_ref, e1_ref, r_ref, r_ref, COEF_A, 1.0)
    def column(out_ref, left, right, plus, by, times, n):
        down = pl.ds(n * BLK, cols - n * BLK)
        value = by * plus(down, block(n)) + times * dot(left[down, :], right[:, block(n)])
        value = value.astype(BF16)
        out_ref[down, block(n)] = value
        for i in range(n + 1, RING):
            out_ref[block(n), block(i)] = value[(i - n) * BLK : (i - n + 1) * BLK, :].T

    def second(n):
        def plus(down, right):
            return a1_ref[down, right].astype(F32)

        column(e2_ref, a1_ref, a1_ref, plus, COEF_B, COEF_C, n)


    factor = math.sqrt(total_rows) * scale
    for n in range(RING):
        if n < 2:
            for later in range(n, RING if n else 1):
                second(later)

        def plus(down, right):
            return e1_ref[down, right].astype(F32) + e2_ref[down, right].astype(F32)

        column(e_ref, e1_ref, e2_ref, plus, COEF_A, 1.0, n)

        def update(span):
            value = COEF_A * COEF_A * x_ref[span, block(n)].astype(F32) + dot(
                x_ref[span, :], e_ref[:, block(n)]
            )
            y_ref[span, block(n)] = (factor * value).astype(BF16)

        def home(offset, core):
            return y_ref.at[
                pl.ds(pl.multiple_of((2 * offset + core) * rows, 16), rows), block(n)
            ]

        def back(offset, core):
            remote(
                home(offset, core),
                u_ref.at[mine, :, block(n)],
                out_send.at[2 * offset + core],
                out_recv.at[mine],
                along_p(offset, core),
            ).start()

        for offset in (2, 1, 3, 0):
            update(pl.ds(2 * offset * rows, 2 * rows))
            if offset:
                back(offset, 0)
                back(offset, 1)
            else:
                back(0, 1 - c)
                pltpu.make_async_copy(home(0, c), u_ref.at[mine, :, block(n)], local_sem.at[1]).start()

    for copy in sent:
        copy.wait_send()

    @pl.when(c == 1)
    def _():
        for offset in range(1, n_groups):
            for core in (0, 1):
                tell(offset, core).wait_send()

    for offset in range(1, n_groups):
        other = lax.rem(group + offset, n_groups)
        remote(
            tab_ref.at[other], tab_ref.at[other], tab_send.at[0], tab_recv.at[other], d
        ).wait_recv()
    sub = lax.broadcasted_iota(jnp.int32, (8, 128), 0)
    whole = jnp.zeros((8, 128), F32)
    for index in range(n_groups):
        whole = jnp.where(sub == index, tab_ref[index], whole)
    whole_ref[...] = whole

    def all_columns(other, offset, core):
        return remote(
            y_ref.at[pl.ds(pl.multiple_of((2 * offset + core) * rows, 16), rows)],
            u_ref.at[other],
            out_send.at[2 * offset + core],
            out_recv.at[other],
            d,
        )

    pltpu.make_async_copy(y_ref.at[pl.ds(0, rows)], u_ref.at[mine], local_sem.at[1]).wait()
    for offset in range(1, RING):
        all_columns(c * RING + lax.rem(p + offset, RING), 0, 0).wait_recv()
    for index in range(RING):
        all_columns((1 - c) * RING + index, 0, 0).wait_recv()
    for offset, core in ((2, 0), (2, 1), (1, 0), (1, 1), (3, 0), (3, 1), (0, 1 - c)):
        all_columns(mine, offset, core).wait_send()


def finish(n_groups, u_ref, whole_ref, owners_ref, update_ref, table_ref, owned_ref, sem):
    mats = u_ref.shape[0]
    copies = [
        pltpu.make_async_copy(u_ref.at[m], update_ref.at[0, m], sem.at[m]) for m in range(mats)
    ]
    for copy in copies:
        copy.start()
    table = whole_ref[...][0:n_groups, 0:mats]
    table_ref[...] = table
    sub = lax.broadcasted_iota(jnp.int32, table.shape, 0)
    mask = (sub == lax.axis_index("expert")) & (owners_ref[...] == lax.axis_index("dp") // 4)
    hit = jnp.sum(jnp.where(mask, table, 0.0), axis=0, keepdims=True)
    owned_ref[...] = jnp.sum(hit, axis=1, keepdims=True)
    for copy in copies:
        copy.wait()


def body(gradients, owners):
    _, mats, rows, cols = gradients.shape
    n_groups = lax.axis_size("expert")
    total_rows = rows * lax.axis_size("dp")
    any_space = pl.BlockSpec(memory_space=pl.ANY)
    vmem = pl.BlockSpec(memory_space=pltpu.VMEM)
    full = pltpu.VMEM((cols, cols), BF16)
    dma = pltpu.SemaphoreType.DMA
    stacks = [len(tiles(stage)) * TILE for stage in STAGES]
    moved, whole = pl.pallas_call(
        functools.partial(kernel, total_rows, n_groups),
        out_shape=(
            pltpu.VMEM((mats, rows, cols), BF16),
            jax.ShapeDtypeStruct((8, 128), F32),
        ),
        in_specs=[any_space],
        out_specs=(vmem, vmem),
        scratch_shapes=[
            pltpu.VMEM((mats * rows, cols), BF16),
            tuple(pltpu.VMEM((stack, TILE), BF16) for stack in stacks),
            tuple(pltpu.VMEM((RING - 1, stack // RING, TILE), BF16) for stack in stacks),
            tuple(pltpu.VMEM((stack, TILE), BF16) for stack in stacks),
            pltpu.VMEM((RING, 8, 128), F32),
            full,
            pltpu.VMEM((3 * BLK, 3 * BLK), F32),
            full,
            full,
            full,
            full,
            full,
            pltpu.VMEM((mats * rows, cols), BF16),
            pltpu.VMEM((2 * RING, 8, 128), F32),
            pltpu.VMEM((n_groups, 8, 128), F32),
            pltpu.SemaphoreType.REGULAR,
            dma((2,)),
            dma((len(STAGES), 2 * RING)),
            dma((len(STAGES), 2 * RING)),
            dma((len(STAGES), RING - 1)),
            dma((len(STAGES), RING - 1)),
            dma((len(STAGES), RING - 1)),
            dma((len(STAGES), RING)),
            dma((RING - 1,)),
            dma((RING,)),
            dma((2 * RING,)),
            dma((2 * RING,)),
            dma((2 * RING - 1,)),
            dma((2 * RING,)),
            dma((2 * (n_groups - 1),)),
            dma((n_groups,)),
        ],
        compiler_params=pltpu.CompilerParams(
            collective_id=0, has_side_effects=True, vmem_limit_bytes=40 * 1024 * 1024
        ),
    )(pltpu.with_memory_space_constraint(gradients, pltpu.HBM))
    return pl.pallas_call(
        functools.partial(finish, n_groups),
        out_shape=(
            jax.ShapeDtypeStruct(gradients.shape, BF16),
            jax.ShapeDtypeStruct((n_groups, mats), F32),
            jax.ShapeDtypeStruct((1, 1), F32),
        ),
        in_specs=[vmem, vmem, vmem],
        out_specs=(any_space, vmem, vmem),
        scratch_shapes=[dma((mats,))],
        compiler_params=pltpu.CompilerParams(vmem_limit_bytes=4 * 1024 * 1024),
    )(moved, whole, owners)


def solution(mesh):
    placed = (P("expert", None, "dp", None), P("expert", None))
    return jax.shard_map(
        body,
        mesh=mesh,
        in_specs=placed,
        out_specs=(P("expert", None, "dp", None), P(), P("expert", "dp")),
        check_vma=False,
    )
```

```python
import functools
import math

import jax
import jax.numpy as jnp
from jax import lax
from jax.experimental import pallas as pl
from jax.experimental.pallas import tpu as pltpu
from jax.sharding import PartitionSpec as P

COEF_A = 3.4445
COEF_B = -4.775
COEF_C = 2.0315

RING = 4
BLK = 256
TILE = 128
STAGES = (((0, BLK), (BLK, BLK)), ((2 * BLK, BLK),), ((3 * BLK, TILE),), ((3 * BLK + TILE, TILE),))
FIRST_STAGES = len([stage for stage in STAGES if sum(stage[-1]) <= 3 * BLK])


def tiles(stage):
    first = stage[0][0] // TILE
    last = sum(stage[-1]) // TILE
    return [(i, j) for i in range(first, last) for j in range(i + 1)]


F32 = jnp.float32
BF16 = jnp.bfloat16


def dot(a, b):
    return lax.dot_general(a, b, (((1,), (0,)), ((), ())), preferred_element_type=F32)


def dot_t(a, b):
    return lax.dot_general(a, b, (((0,), (0,)), ((), ())), preferred_element_type=F32)


def kernel(
    total_rows,
    n_groups,
    g_ref,
    u_ref,
    whole_ref,
    x_ref,
    piece_refs,
    got_refs,
    all_refs,
    tr_ref,
    s_ref,
    t_ref,
    e1_ref,
    r_ref,
    a1_ref,
    e2_ref,
    e_ref,
    y_ref,
    rms_ref,
    tab_ref,
    go_sem,
    local_sem,
    in_send,
    in_recv,
    rs_send,
    rs_recv,
    ag_send,
    ag_recv,
    tr_send,
    tr_recv,
    out_send,
    out_recv,
    rms_send,
    rms_recv,
    tab_send,
    tab_recv,
    whole_send,
    whole_recv,
):
    rows = g_ref.shape[2]
    cols = g_ref.shape[3]
    d = lax.axis_index("dp")
    group = lax.axis_index("expert")
    c = lax.rem(d, 2)
    x = lax.rem(d // 2, RING)
    y = d // (2 * RING)
    p = jnp.where(c == 0, x, y)
    q = jnp.where(c == 0, y, x)
    p_stride = jnp.where(c == 0, 2, 2 * RING)
    q_stride = jnp.where(c == 0, 2 * RING, 2)
    chip = d - c
    mine = c * RING + p

    def along_p(offset, core):
        return chip + (lax.rem(p + offset, RING) - p) * p_stride + core

    def along_q(offset, core):
        return chip + (lax.rem(q + offset, RING) - q) * q_stride + core

    def remote(src, dst, send, recv, dp, to_group=group):
        return pltpu.make_async_remote_copy(
            src_ref=src,
            dst_ref=dst,
            send_sem=send,
            recv_sem=recv,
            device_id=(dp, to_group),
            device_id_type=pl.DeviceIdType.MESH,
        )

    barrier = pltpu.get_barrier_semaphore()

    def greet(sem, dp, to_group=group):
        pl.semaphore_signal(
            sem, inc=1, device_id=(dp, to_group), device_id_type=pl.DeviceIdType.MESH
        )

    def greet_unless_one(dp):
        @pl.when(dp != 1)
        def _():
            greet(barrier, dp)

    for offset in range(1, RING):
        for along in (along_p, along_q):
            greet(barrier, along(offset, 0))
            greet_unless_one(along(offset, 1))
    greet_unless_one(chip + 1 - c)

    own = pltpu.make_async_copy(
        g_ref.at[0, mine], x_ref.at[pl.ds(pl.multiple_of(c * rows, 16), rows)], local_sem.at[0]
    )
    own.start()

    @pl.when(d != 1)
    def _():
        pl.semaphore_wait(barrier, 4 * (RING - 1) + 1)

    @pl.when(d == 0)
    def _():
        greet(go_sem, 1)

    @pl.when(d == 1)
    def _():
        pl.semaphore_wait(go_sem, 1)

    parts = [pl.ds(stage[0][0], sum(stage[-1]) - stage[0][0]) for stage in STAGES]

    def slot(offset, core, part):
        return x_ref.at[pl.ds(pl.multiple_of((2 * offset + core) * rows, 16), rows), part]

    sent = []
    for number, part in enumerate(parts):
        for offset in (2, 1, 3, 0):
            back = (RING - offset) % RING
            if offset:
                copy = remote(
                    g_ref.at[0, c * RING + lax.rem(p + back, RING), :, part],
                    slot(offset, c, part),
                    in_send.at[number, 2 * offset],
                    in_recv.at[number, 2 * offset + c],
                    along_p(back, c),
                )
                copy.start()
                sent.append(copy)
            copy = remote(
                g_ref.at[0, (1 - c) * RING + lax.rem(q + back, RING), :, part],
                slot(offset, c, part),
                in_send.at[number, 2 * offset + 1],
                in_recv.at[number, 2 * offset + c],
                along_q(back, 1 - c),
            )
            copy.start()
            sent.append(copy)

    @pl.when(d == 1)
    def _():
        for offset in range(1, n_groups):
            greet(barrier, d, lax.rem(group + offset, n_groups))

    def arrive(number, offsets=(0, 1, 3, 2)):
        part = parts[number]
        slots = [(offset, core) for offset in offsets for core in (0, 1) if offset]
        if 0 in offsets:
            slots.insert(0, (0, 1 - c))
        for offset, core in slots:
            remote(
                g_ref.at[0, 0, :, part],
                slot(offset, core, part),
                in_send.at[number, 0],
                in_recv.at[number, 2 * offset + core],
                d,
            ).wait_recv()

    def partial_gram(number):
        total = jnp.zeros((1, 1), F32)
        places = tiles(STAGES[number])
        chunks = [((0, 1, 3, 2), 0, 2 * RING)]
        if number == len(STAGES) - 1:
            chunks = [((0, 1), 0, 4), ((3,), 6, 2), ((2,), 4, 2)]
        for first, count in STAGES[number]:
            value = None
            for offsets, start, size in chunks:
                if number == len(STAGES) - 1 and first == STAGES[number][0][0]:
                    arrive(number, offsets)
                here = pl.ds(start * rows, size * rows)
                term = dot_t(x_ref[here, pl.ds(first, count)], x_ref[here, pl.ds(0, first + count)])
                value = term if value is None else value + term
            diag = lax.broadcasted_iota(jnp.int32, (count, count), 0) == lax.broadcasted_iota(
                jnp.int32, (count, count), 1
            )
            line = jnp.sum(jnp.where(diag, value[:, first:], 0.0), axis=0, keepdims=True)
            total += jnp.sum(line, axis=1, keepdims=True)
            for down in range(0, count, TILE):
                i = (first + down) // TILE
                for j in range(i + 1):
                    piece_refs[number][pl.ds(places.index((i, j)) * TILE, TILE)] = value[
                        down : down + TILE, j * TILE : (j + 1) * TILE
                    ].astype(BF16)
        return total

    def quarter(number, k):
        share = len(tiles(STAGES[number])) * TILE // RING
        return pl.ds(pl.multiple_of(k * share, share), share)

    def scatter(number):
        for offset in (2, 1, 3):
            copy = remote(
                piece_refs[number].at[quarter(number, lax.rem(q + offset, RING))],
                got_refs[number].at[RING - 1 - offset],
                rs_send.at[number, offset - 1],
                rs_recv.at[number, RING - 1 - offset],
                along_q(offset, c),
            )
            copy.start()
            sent.append(copy)

    def add_up(number):
        got_ref = got_refs[number]
        here = quarter(number, q)
        for index in range(RING - 1):
            remote(
                got_ref.at[index],
                got_ref.at[index],
                rs_send.at[number, 0],
                rs_recv.at[number, index],
                d,
            ).wait_recv()
        all_refs[number][here] = (
            (piece_refs[number][here].astype(F32) + got_ref[0].astype(F32))
            + (got_ref[1].astype(F32) + got_ref[2].astype(F32))
        ).astype(BF16)
        for offset in (2, 1, 3):
            copy = remote(
                all_refs[number].at[here],
                all_refs[number].at[here],
                ag_send.at[number, offset - 1],
                ag_recv.at[number, q],
                along_q(offset, c),
            )
            copy.start()
            sent.append(copy)

    def collect(number):
        for offset in (1, 3, 2):
            k = lax.rem(q + offset, RING)
            part = all_refs[number].at[quarter(number, k)]
            remote(part, part, ag_send.at[number, 0], ag_recv.at[number, k], d).wait_recv()

    own.wait()
    total = jnp.zeros((1, 1), F32)
    for number in range(len(STAGES)):
        if number < len(STAGES) - 1:
            arrive(number)
        total += partial_gram(number)
        scatter(number)
    tr_ref[q] = jnp.broadcast_to(total, (8, 128))
    for offset in (2, 1, 3):
        copy = remote(
            tr_ref.at[q], tr_ref.at[q], tr_send.at[offset - 1], tr_recv.at[q], along_q(offset, c)
        )
        copy.start()
        sent.append(copy)
    for number in range(len(STAGES)):
        add_up(number)

    for offset in (1, 3, 2):
        k = lax.rem(q + offset, RING)
        remote(tr_ref.at[k], tr_ref.at[k], tr_send.at[0], tr_recv.at[k], d).wait_recv()
    trace = ((tr_ref[0] + tr_ref[1]) + (tr_ref[2] + tr_ref[3]))[0:1, 0:1]
    scale = 1.0 / jnp.sqrt(trace + 1e-06)
    rms = jnp.sqrt(trace / (total_rows * cols))
    rms_ref[mine] = jnp.broadcast_to(rms, (8, 128))
    number = 0
    for offset in range(RING):
        for core in (c, 1 - c):
            if offset == 0 and core is c:
                continue
            copy = remote(
                rms_ref.at[mine],
                rms_ref.at[mine],
                rms_send.at[number],
                rms_recv.at[mine],
                along_p(offset, core),
            )
            copy.start()
            sent.append(copy)
            number += 1

    square = scale * scale

    def block(i):
        return pl.ds(i * BLK, BLK)

    def unpack(number):
        collect(number)
        for place, (i, j) in enumerate(tiles(STAGES[number])):
            down, right = pl.ds(i * TILE, TILE), pl.ds(j * TILE, TILE)
            one = all_refs[number][pl.ds(place * TILE, TILE)].astype(F32) * square
            one = one.astype(BF16)
            s_ref[down, right] = one
            if i != j:
                s_ref[right, down] = one.T

    for number in range(FIRST_STAGES):
        unpack(number)

    for offset in range(1, RING):
        other = c * RING + lax.rem(p + offset, RING)
        remote(rms_ref.at[other], rms_ref.at[other], rms_send.at[0], rms_recv.at[other], d).wait_recv()
    for index in range(RING):
        other = (1 - c) * RING + index
        remote(rms_ref.at[other], rms_ref.at[other], rms_send.at[0], rms_recv.at[other], d).wait_recv()
    lane = lax.broadcasted_iota(jnp.int32, (8, 128), 1)
    line = jnp.zeros((8, 128), F32)
    for index in range(2 * RING):
        line = jnp.where(lane == index, rms_ref[index], line)
    tab_ref[group] = line

    def tell(offset):
        return remote(
            tab_ref.at[group],
            tab_ref.at[group],
            tab_send.at[offset - 1],
            tab_recv.at[group],
            d,
            lax.rem(group + offset, n_groups),
        )

    @pl.when(d == 1)
    def _():
        pl.semaphore_wait(barrier, n_groups - 1)
        for offset in range(1, n_groups):
            tell(offset).start()

    def along_row():
        targets = [along_q(offset, core) for offset in range(1, RING) for core in (0, 1)]
        return [
            remote(whole_ref, whole_ref, whole_send.at[number], whole_recv, dp)
            for number, dp in enumerate([d - 1, *targets])
        ]

    def along_column():
        return [
            remote(whole_ref, whole_ref, whole_send.at[2 * RING + up], whole_recv, d + 2 * RING * up)
            for up in range(1, RING)
        ]

    def have_table():
        remote(whole_ref, whole_ref, whole_send.at[0], whole_recv, d).wait_recv()

    def share_table():
        for offset in range(1, n_groups):
            other = lax.rem(group + offset, n_groups)
            remote(
                tab_ref.at[other], tab_ref.at[other], tab_send.at[0], tab_recv.at[other], d
            ).wait_recv()
        sub = lax.broadcasted_iota(jnp.int32, (8, 128), 0)
        whole = jnp.zeros((8, 128), F32)
        for index in range(n_groups):
            whole = jnp.where(sub == index, tab_ref[index], whole)
        whole_ref[...] = whole
        for copy in along_row():
            copy.start()

    early = 3 * BLK
    for i in range(RING - 1):
        wide = pl.ds(0, (i + 1) * BLK)
        t_ref[block(i), wide] = COEF_B * s_ref[block(i), wide].astype(F32) + COEF_C * dot(
            s_ref[block(i), pl.ds(0, early)], s_ref[pl.ds(0, early), wide]
        )
    for number in range(FIRST_STAGES, len(STAGES)):
        unpack(number)

    def turn_over(out_ref, i, value):
        value = value.astype(BF16)
        out_ref[block(i), pl.ds(0, (i + 1) * BLK)] = value
        for j in range(i):
            out_ref[block(j), block(i)] = value[:, j * BLK : (j + 1) * BLK].T

    def product(out_ref, left, right, plus, by, times, first=0):
        for i in range(first, RING):
            wide = pl.ds(0, (i + 1) * BLK)
            value = by * plus[block(i), wide].astype(F32) + times * dot(
                left[block(i), :], right[:, wide]
            )
            turn_over(out_ref, i, value)

    for i in range(RING - 1):
        wide = pl.ds(0, (i + 1) * BLK)
        value = t_ref[block(i), wide] + COEF_C * dot(s_ref[block(i), block(3)], s_ref[block(3), wide])
        turn_over(e1_ref, i, value)
    product(e1_ref, s_ref, s_ref, s_ref, COEF_B, COEF_C, RING - 1)

    product(r_ref, e1_ref, s_ref, s_ref, COEF_A, 1.0)
    product(a1_ref, e1_ref, r_ref, r_ref, COEF_A, 1.0)
    def column(out_ref, left, right, plus, by, times, n):
        down = pl.ds(n * BLK, cols - n * BLK)
        value = by * plus(down, block(n)) + times * dot(left[down, :], right[:, block(n)])
        value = value.astype(BF16)
        out_ref[down, block(n)] = value
        for i in range(n + 1, RING):
            out_ref[block(n), block(i)] = value[(i - n) * BLK : (i - n + 1) * BLK, :].T

    def second(n):
        def plus(down, right):
            return a1_ref[down, right].astype(F32)

        column(e2_ref, a1_ref, a1_ref, plus, COEF_B, COEF_C, n)


    factor = math.sqrt(total_rows) * scale
    for n in range(RING):
        if n < 2:
            for later in range(n, RING if n else 1):
                second(later)

        def plus(down, right):
            return e1_ref[down, right].astype(F32) + e2_ref[down, right].astype(F32)

        column(e_ref, e1_ref, e2_ref, plus, COEF_A, 1.0, n)

        def update(span):
            value = COEF_A * COEF_A * x_ref[span, block(n)].astype(F32) + dot(
                x_ref[span, :], e_ref[:, block(n)]
            )
            y_ref[span, block(n)] = (factor * value).astype(BF16)

        def home(offset, core):
            return y_ref.at[
                pl.ds(pl.multiple_of((2 * offset + core) * rows, 16), rows), block(n)
            ]

        def back(offset, core):
            remote(
                home(offset, core),
                u_ref.at[mine, :, block(n)],
                out_send.at[2 * offset + core],
                out_recv.at[mine],
                along_p(offset, core),
            ).start()

        for offset in (2, 1, 3, 0):
            update(pl.ds(2 * offset * rows, 2 * rows))
            if offset:
                back(offset, 0)
                back(offset, 1)
            else:
                back(0, 1 - c)
                pltpu.make_async_copy(home(0, c), u_ref.at[mine, :, block(n)], local_sem.at[1]).start()
        if n == 1:
            pl.when(d == 1)(share_table)

    for copy in sent:
        copy.wait_send()

    @pl.when((y == 0) & (d != 1))
    def _():
        have_table()

    @pl.when(y == 0)
    def _():
        for copy in along_column():
            copy.start()

    @pl.when(y != 0)
    def _():
        have_table()

    @pl.when(y == 0)
    def _():
        for copy in along_column():
            copy.wait_send()

    @pl.when(d == 1)
    def _():
        for copy in along_row():
            copy.wait_send()
        for offset in range(1, n_groups):
            tell(offset).wait_send()

    def all_columns(other, offset, core):
        return remote(
            y_ref.at[pl.ds(pl.multiple_of((2 * offset + core) * rows, 16), rows)],
            u_ref.at[other],
            out_send.at[2 * offset + core],
            out_recv.at[other],
            d,
        )

    pltpu.make_async_copy(y_ref.at[pl.ds(0, rows)], u_ref.at[mine], local_sem.at[1]).wait()
    for offset in range(1, RING):
        all_columns(c * RING + lax.rem(p + offset, RING), 0, 0).wait_recv()
    for index in range(RING):
        all_columns((1 - c) * RING + index, 0, 0).wait_recv()
    for offset, core in ((2, 0), (2, 1), (1, 0), (1, 1), (3, 0), (3, 1), (0, 1 - c)):
        all_columns(mine, offset, core).wait_send()


def finish(n_groups, u_ref, whole_ref, owners_ref, update_ref, table_ref, owned_ref, sem):
    mats = u_ref.shape[0]
    copies = [
        pltpu.make_async_copy(u_ref.at[m], update_ref.at[0, m], sem.at[m]) for m in range(mats)
    ]
    for copy in copies:
        copy.start()
    table = whole_ref[...][0:n_groups, 0:mats]
    table_ref[...] = table
    sub = lax.broadcasted_iota(jnp.int32, table.shape, 0)
    mask = (sub == lax.axis_index("expert")) & (owners_ref[...] == lax.axis_index("dp") // 4)
    hit = jnp.sum(jnp.where(mask, table, 0.0), axis=0, keepdims=True)
    owned_ref[...] = jnp.sum(hit, axis=1, keepdims=True)
    for copy in copies:
        copy.wait()


def body(gradients, owners):
    _, mats, rows, cols = gradients.shape
    n_groups = lax.axis_size("expert")
    total_rows = rows * lax.axis_size("dp")
    any_space = pl.BlockSpec(memory_space=pl.ANY)
    vmem = pl.BlockSpec(memory_space=pltpu.VMEM)
    full = pltpu.VMEM((cols, cols), BF16)
    dma = pltpu.SemaphoreType.DMA
    stacks = [len(tiles(stage)) * TILE for stage in STAGES]
    moved, whole = pl.pallas_call(
        functools.partial(kernel, total_rows, n_groups),
        out_shape=(
            pltpu.VMEM((mats, rows, cols), BF16),
            jax.ShapeDtypeStruct((8, 128), F32),
        ),
        in_specs=[any_space],
        out_specs=(vmem, vmem),
        scratch_shapes=[
            pltpu.VMEM((mats * rows, cols), BF16),
            tuple(pltpu.VMEM((stack, TILE), BF16) for stack in stacks),
            tuple(pltpu.VMEM((RING - 1, stack // RING, TILE), BF16) for stack in stacks),
            tuple(pltpu.VMEM((stack, TILE), BF16) for stack in stacks),
            pltpu.VMEM((RING, 8, 128), F32),
            full,
            pltpu.VMEM((3 * BLK, 3 * BLK), F32),
            full,
            full,
            full,
            full,
            full,
            pltpu.VMEM((mats * rows, cols), BF16),
            pltpu.VMEM((2 * RING, 8, 128), F32),
            pltpu.VMEM((n_groups, 8, 128), F32),
            pltpu.SemaphoreType.REGULAR,
            dma((2,)),
            dma((len(STAGES), 2 * RING)),
            dma((len(STAGES), 2 * RING)),
            dma((len(STAGES), RING - 1)),
            dma((len(STAGES), RING - 1)),
            dma((len(STAGES), RING - 1)),
            dma((len(STAGES), RING)),
            dma((RING - 1,)),
            dma((RING,)),
            dma((2 * RING,)),
            dma((2 * RING,)),
            dma((2 * RING - 1,)),
            dma((2 * RING,)),
            dma((n_groups - 1,)),
            dma((n_groups,)),
            dma((3 * RING,)),
            dma(()),
        ],
        compiler_params=pltpu.CompilerParams(
            collective_id=0, has_side_effects=True, vmem_limit_bytes=40 * 1024 * 1024
        ),
    )(pltpu.with_memory_space_constraint(gradients, pltpu.HBM))
    return pl.pallas_call(
        functools.partial(finish, n_groups),
        out_shape=(
            jax.ShapeDtypeStruct(gradients.shape, BF16),
            jax.ShapeDtypeStruct((n_groups, mats), F32),
            jax.ShapeDtypeStruct((1, 1), F32),
        ),
        in_specs=[vmem, vmem, vmem],
        out_specs=(any_space, vmem, vmem),
        scratch_shapes=[dma((mats,))],
        compiler_params=pltpu.CompilerParams(vmem_limit_bytes=4 * 1024 * 1024),
    )(moved, whole, owners)


def solution(mesh):
    placed = (P("expert", None, "dp", None), P("expert", None))
    return jax.shard_map(
        body,
        mesh=mesh,
        in_specs=placed,
        out_specs=(P("expert", None, "dp", None), P(), P("expert", "dp")),
        check_vma=False,
    )
```
